1024 devices in a mesh: orb: 128 (over z, x), aux: 8 (over y, core).
Axes of the slice: x: 4, y: 4, z: 32, core: 2. Of those that a mesh axis runs over, the one named last changes fastest.
Arguments:
- integrals: bfloat16 [128, 8192, 192], P('aux', 'orb'), may hold values from -0.4375 to 0.4375
- coefficients: bfloat16 [8192, 1024], P('orb'), may hold values from -0.09375 to 0.09375
- metric: bfloat16 [128, 128], replicated, may hold values from -0.5 to 0.5
- screening: int32 [8, 128, 3], P('aux', 'orb'), may hold values 0 or 1
Outputs:
- exchange_band: float32 [8192, 192], P('orb')
The draws below stay inside these ranges and needn't reach their ends.
All inputs are finite; a program needn't handle non-finite values. No bound on the sum of `screening` on one device may be relied on, other than what follows from the above.
Results may differ from the reference program's by a relative error of at most 0.00031.
Values may be sent and summed in bfloat16 or wider, within the bound.
A program may use at most 32 MiB of HBM per device.

```python
import jax
import jax.numpy as jnp
from jax import lax

NOCC = 1024
MU_DEV = 64
AUX_DEV = 16
NAUX = 128
NBLK = 128
NABLK = 8
NBAS = 8192
N_ORB = 128


def place_ends(array, key, low, high):
    extent = array.shape
    place = [jax.random.randint(jax.random.fold_in(key, axis), (), 0, extent[axis]) for axis in range(len(extent))]
    array = array.at[tuple(place)].set(low)
    longest = extent.index(max(extent))
    place[longest] = (place[longest] + 1) % extent[longest]
    return array.at[tuple(place)].set(high)


def block_scale(own_key, shape, pieces, smallest, top_value):
    def one(axis_at, shards_of):
        steps = jax.random.uniform(jax.random.fold_in(jax.random.fold_in(own_key, 6), axis_at), (shards_of,), jnp.float32, smallest / len(pieces), top_value / len(pieces))
        return jnp.repeat(jnp.exp(steps), shape[axis_at] // shards_of).reshape((-1,) + (1,) * (len(shape) - axis_at - 1))

    factor_of = one(*pieces[0])
    for cut in pieces[1:]:
        factor_of = factor_of * one(*cut)
    return factor_of


def bell_draw(key, shape, width, bound, cuts=(), dtype=jnp.bfloat16):
    drawn = jax.random.normal(key, shape, jnp.float32) * width
    if len(cuts) > 0:
        drawn = block_scale(key, shape, cuts, -0.22, 0.18) * drawn
    return jnp.clip(drawn, min=-bound, max=bound).astype(dtype)


def setup_inputs(seed: int = 0) -> dict:
    streams_of = jax.random.split(jax.random.key(seed), 5)
    return {
        "integrals": bell_draw(streams_of[0], (NAUX, NBAS, 3 * MU_DEV), (3 * MU_DEV) ** -0.5, 0.4375, ((0, 8), (1, 128))),
        "coefficients": bell_draw(streams_of[1], (NBAS, NOCC), (4 * NOCC) ** -0.5, 0.09375, ((0, 128),)),
        "metric": bell_draw(streams_of[2], (NAUX, NAUX), NAUX ** -0.5, 0.5),
        "screening": place_ends((jax.random.randint(streams_of[3], (NABLK, NBLK, 3), 0, 3) < 2).astype(jnp.int32), jax.random.fold_in(streams_of[3], 1), 0, 1),
    }


def pair_block(left, right):
    return jnp.einsum('pmi,pni->mn', left.astype(jnp.float32), right.astype(jnp.float32))


def reference(integrals, coefficients, metric, screening):
    coef = coefficients.reshape(N_ORB, MU_DEV, NOCC)
    window = jnp.concatenate([jnp.roll(coef, 1, 0), coef, jnp.roll(coef, -1, 0)], axis=1)
    gate = jnp.repeat(jnp.repeat(screening, AUX_DEV, axis=0), MU_DEV, axis=2)
    ints = integrals.reshape(NAUX, N_ORB, MU_DEV, 3 * MU_DEV)
    metric_wide = metric.astype(jnp.float32)

    def panel(index):
        block_ints = lax.dynamic_index_in_dim(ints, index, 1, keepdims=False)
        block_gate = lax.dynamic_index_in_dim(gate, index, 1, keepdims=False)
        masked = block_ints * block_gate[:, None, :].astype(jnp.bfloat16)
        rows = lax.dynamic_index_in_dim(window, index, 0, keepdims=False)
        half = jnp.dot(masked.reshape(NAUX * MU_DEV, 3 * MU_DEV), rows, preferred_element_type=jnp.float32)
        half = half.astype(jnp.bfloat16).reshape(NAUX, MU_DEV, NOCC)
        fitted = jnp.einsum('pq,qmi->pmi', metric_wide, half.astype(jnp.float32))
        return fitted.astype(jnp.bfloat16)

    first = panel(0)

    def advance(previous, index):
        current = panel(index)
        return current, (pair_block(current, current), pair_block(previous, current))

    last, (diagonals, uppers) = lax.scan(advance, first, jnp.arange(1, N_ORB).astype(jnp.int32))
    diag_all = jnp.concatenate([pair_block(first, first)[None], diagonals], axis=0)
    upper_all = jnp.concatenate([uppers, pair_block(last, first)[None]], axis=0)
    lower_all = jnp.transpose(jnp.roll(upper_all, 1, 0), (0, 2, 1))
    band = jnp.concatenate([lower_all, diag_all, upper_all], axis=2)
    return band.reshape(NBAS, 3 * MU_DEV)
```

```python
import functools

import jax
import jax.numpy as jnp
from jax import lax
from jax.experimental import pallas as pl
from jax.experimental.pallas import tpu as pltpu
from jax.sharding import PartitionSpec as P

MESH = pl.DeviceIdType.MESH
F32 = jnp.float32
BF16 = jnp.bfloat16
HEAD = (0, 1, 4, 5)
TAIL = (2, 3)
CHUNKS = ((0, 2), (2, 2), (4, 2))


def nn(a, b):
    return lax.dot_general(a, b, (((1,), (0,)), ((), ())), preferred_element_type=F32)


def nt(a, b):
    return lax.dot_general(a, b, (((1,), (1,)), ((), ())), preferred_element_type=F32)


def split(x):
    high = x.astype(BF16)
    return high, (x - high.astype(F32)).astype(BF16)


def iota(shape, dim):
    return lax.broadcasted_iota(jnp.int32, shape, dim)


def fold(x):
    return jnp.concatenate([x[16 * p : 16 * p + 16] for p in range(16)], axis=1)


def kernel(
    n_orb,
    a_ref, c_ref, m_ref, s_ref, o_ref,
    av, cb, ag, mk, psend, precv, ghi, glo, gn, sp_hi, sp_lo, hh, ht, kp, rs, ob,
    load_sem, ag_send, ag_recv, sib_send, sib_recv, c_send, c_recv, g_send, g_recv, r_send, r_recv, b_send, b_recv,
):
    orb = lax.axis_index("orb")
    aux = lax.axis_index("aux")
    y = lax.div(aux, 2)
    core = lax.rem(aux, 2)
    sibling = (orb, 2 * y + 1 - core)
    up = (orb, lax.rem(aux + 2, 8))
    down = (orb, lax.rem(aux + 6, 8))
    after = (lax.rem(orb + 1, n_orb), aux)
    before = (lax.rem(orb + n_orb - 1, n_orb), aux)
    peers = [(orb, lax.rem(aux + j, 8)) for j in range(1, 8)]

    def remote(src, dst, send, recv, target):
        return pltpu.make_async_remote_copy(
            src_ref=src, dst_ref=dst, send_sem=send, recv_sem=recv, device_id=target, device_id_type=MESH
        )

    load_a0 = pltpu.make_async_copy(a_ref.at[:, pl.ds(0, 32), :], av.at[:, pl.ds(0, 32), :], load_sem.at[0])
    load_a1 = pltpu.make_async_copy(a_ref.at[:, pl.ds(32, 32), :], av.at[:, pl.ds(32, 32), :], load_sem.at[1])
    load_c = pltpu.make_async_copy(c_ref, cb.at[2], load_sem.at[2])
    load_a0.start()
    load_c.start()
    load_a1.start()

    barrier = pltpu.get_barrier_semaphore()
    for target in peers + [after, before]:
        pl.semaphore_signal(barrier, inc=1, device_id=target, device_id_type=MESH)

    gate = [s_ref[0, 0, k].astype(F32) for k in range(3)]
    lane = iota((1, 128), 1)
    head_mask = jnp.where(lane < 64, gate[0], gate[1]).astype(BF16)
    rows = pl.ds(pl.multiple_of(256 * y, 256), 256)

    def pack_head(group):
        piece = av[:, 16 * group : 16 * group + 16, 0:128].reshape(256, 128)
        ag[HEAD[group], rows, :] = piece * head_mask

    def pack_tail(which):
        shape = (64, 128)
        low = jnp.where(iota(shape, 0) == iota(shape, 1), gate[2], 0.0).astype(BF16)
        high = jnp.where(iota(shape, 0) + 64 == iota(shape, 1), gate[2], 0.0).astype(BF16)
        first = av[:, 16 * which : 16 * which + 16, 128:192].reshape(256, 64)
        second = av[:, 16 * which + 32 : 16 * which + 48, 128:192].reshape(256, 64)
        ag[TAIL[which], rows, :] = (nn(first, low) + nn(second, high)).astype(BF16)

    load_a0.wait()
    pack_head(0)
    pack_head(1)
    pl.semaphore_wait(barrier, 9)

    def slot(c, index, first, count):
        t, n = CHUNKS[c]
        return ag.at[pl.ds(t, n), pl.ds(pl.multiple_of(256 * index + first, 128), count), :]

    y_up, y_down = lax.rem(y + 1, 4), lax.rem(y + 3, 4)

    def own(c):
        block = slot(c, y, 0, 256)
        return [
            remote(block, block, ag_send.at[c, 0], ag_recv.at[c, 0], up),
            remote(block, block, ag_send.at[c, 1], ag_recv.at[c, 1], down),
        ]

    def relay(c):
        first, second = slot(c, y_down, 0, 128), slot(c, y_up, 128, 128)
        return [
            remote(first, first, ag_send.at[c, 2], ag_recv.at[c, 2], up),
            remote(second, second, ag_send.at[c, 3], ag_recv.at[c, 3], down),
        ]

    owns = [own(c) for c in range(len(CHUNKS))]
    relays = [relay(c) for c in range(len(CHUNKS))]

    def start(copies):
        for copy in copies:
            copy.start()

    start(owns[0])
    load_c.wait()
    coef = [
        remote(cb.at[2], cb.at[1], c_send.at[0], c_recv.at[0], after),
        remote(cb.at[2], cb.at[3], c_send.at[1], c_recv.at[1], before),
    ]
    coef_on = [
        remote(cb.at[1], cb.at[0], c_send.at[2], c_recv.at[2], after),
        remote(cb.at[3], cb.at[4], c_send.at[3], c_recv.at[3], before),
    ]
    start(coef)
    load_a1.wait()
    pack_tail(0)
    pack_tail(1)
    start(owns[1])
    pack_head(2)
    pack_head(3)

    metric_rows = m_ref[pl.ds(pl.multiple_of(32 * y, 32), 32), :]
    column = iota((128, 1024), 1)
    wanted = (2 * (column // 256) + core) * 16 + (column // 16) % 16
    spread = jnp.where(iota((128, 1024), 0) == wanted, 1.0, 0.0).astype(BF16)
    for part in range(4):
        row = iota((128, 32), 0) + 128 * part
        holder = core if part < 2 else 1 - core
        pick = jnp.where(iota((128, 32), 1) == holder * 16 + (row // 16) % 16, 1.0, 0.0).astype(BF16)
        picked = nn(pick, metric_rows).astype(BF16)
        wide = nn(picked, spread)
        same = iota((128, 1024), 0) % 16 == iota((128, 1024), 1) % 16
        mk[128 * part : 128 * part + 128, :] = jnp.where(same, wide, 0.0).astype(BF16)

    def arrive(copies):
        for copy in copies:
            copy.wait_recv()

    arrive(coef)
    start(coef_on)
    arrive(owns[0])
    start(relays[0])
    start(owns[2])

    def gram():
        arrive(coef_on)
        left = cb[1:4].reshape(192, 1024)
        for d in range(3):
            right = jnp.concatenate([cb[d], cb[d + 1], cb[d + 2], cb[d + 2]], axis=0)
            lanes = slice(256 * d, 256 * d + 256)
            zero = jnp.zeros((64, 256), BF16)
            for part, dst in zip(split(nt(left, right)), (sp_hi, sp_lo)):
                dst[0, 0:192, lanes] = part
                dst[0, 192:256, lanes] = zero
                dst[1, 0:128, lanes] = part[0:128]
                dst[1, 128:192, lanes] = zero
                dst[1, 192:256, lanes] = part[128:192]

    def sib(c):
        t, n = CHUNKS[c]
        tiles = pl.ds(t, n)
        return remote(psend.at[tiles], precv.at[tiles], sib_send.at[c], sib_recv.at[c], sibling)

    sibs = [sib(c) for c in range(len(CHUNKS))]

    def near(c):
        t, n = CHUNKS[c]
        tiles = pl.ds(t, n)
        return [
            remote(ghi.at[tiles], gn.at[0, tiles], g_send.at[c, 0], g_recv.at[c, 0], after),
            remote(ghi.at[tiles], gn.at[1, tiles], g_send.at[c, 1], g_recv.at[c, 1], before),
        ]

    nears = [near(c) for c in range(len(CHUNKS))]
    kept = {}

    def mix(c):
        t, n = CHUNKS[c]
        arrive(relays[c])
        panel = jnp.concatenate([ag[i] for i in range(t, t + n)], axis=1)
        other = nn(mk[256:512, :], panel)
        for i in range(n):
            psend[t + i] = other[:, 128 * i : 128 * i + 128]
        sibs[c].start()
        mine = nn(mk[0:256, :], panel)
        kept[c] = mine

    def finish(c):
        t, n = CHUNKS[c]
        sibs[c].wait_recv()
        for i in range(n):
            high, low = split(kept[c][:, 128 * i : 128 * i + 128] + precv[t + i])
            ghi[t + i] = high
            glo[t + i] = low
        start(nears[c])

    low_lanes = iota((256, 128), 1) < 64

    def transform(group):
        par, h, t = group // 2, HEAD[group], TAIL[group % 2]
        high = jnp.concatenate([ghi[h], ghi[t]], axis=1)
        low = jnp.concatenate([glo[h], glo[t]], axis=1)
        for d in range(3):
            lanes = slice(256 * d, 256 * d + 256)
            right = sp_hi[par, :, lanes]
            out = nn(high, right) + nn(low, right) + nn(high, sp_lo[par, :, lanes])
            for at, part in enumerate(split(out)):
                row = slice(64 * at + 16 * group, 64 * at + 16 * group + 16)
                hh[d, row, :] = fold(part[:, 0:128])
                end = part[:, 128:256]
                zero = jnp.zeros_like(end)
                ht[d, row, :] = fold(jnp.where(low_lanes, end, zero))
                row = slice(128 + row.start, 128 + row.stop)
                ht[d, row, :] = fold(jnp.where(low_lanes, zero, end))

    def panel_of(ref, tiles):
        return jnp.concatenate([fold(ref[t]) for t in tiles], axis=0)

    def heads(d, ref, tiles):
        out = nt(hh[d], panel_of(ref, tiles))
        return out[0:64] + out[64:128]

    def tails(d, ref):
        out = nt(ht[d], panel_of(ref, TAIL))
        return out[0:64] + out[64:128], out[128:192] + out[192:256]

    mix(0)
    gram()
    arrive(owns[1])
    start(relays[1])
    finish(0)
    arrive(owns[2])
    start(relays[2])
    mix(1)
    finish(1)
    transform(0)
    transform(1)
    mix(2)
    finish(2)
    transform(2)
    transform(3)

    bands = [None, None, None]
    even, odd = tails(1, ghi)
    first = heads(1, ghi, HEAD[:2]) + even + nt(hh[1, 0:64, :], panel_of(glo, HEAD[:2]))
    second = heads(1, ghi, HEAD[2:]) + odd + nt(hh[1, 0:64, :], panel_of(glo, HEAD[2:]))
    first = first + nt(ht[1, 0:64, :], panel_of(glo, TAIL))
    second = second + nt(ht[1, 128:192, :], panel_of(glo, TAIL))
    bands[1] = (first, second)
    for c in range(2):
        arrive(nears[c])
    partial = {}
    for d, ref in ((0, gn.at[0]), (2, gn.at[1])):
        even, odd = tails(d, ref)
        partial[d] = (heads(d, ref, HEAD[:2]) + even, odd)
    arrive(nears[2])
    for d, ref in ((0, gn.at[0]), (2, gn.at[1])):
        bands[d] = (partial[d][0], partial[d][1] + heads(d, ref, HEAD[2:]))
    kp[...] = jnp.concatenate([part for band in bands for part in band], axis=1)

    scatter = []
    for j, target in enumerate(peers):
        src = kp.at[pl.ds(pl.multiple_of(8 * target[1], 8), 8), :]
        scatter.append(remote(src, rs.at[j], r_send.at[j], r_recv.at[j], target))
    start(scatter)
    mine = pl.ds(pl.multiple_of(8 * aux, 8), 8)
    total = kp[mine, :]
    arrive(scatter)
    for j in range(7):
        total = total + rs[j]
    ob[mine, :] = total
    gather = []
    for j, target in enumerate(peers):
        gather.append(remote(ob.at[mine, :], ob.at[mine, :], b_send.at[j], b_recv.at[j], target))
    start(gather)
    arrive(gather)
    store = pltpu.make_async_copy(ob, o_ref, load_sem.at[3])
    store.start()
    sent = coef + coef_on + sibs + scatter + gather
    for copies in owns + relays + nears:
        sent = sent + copies
    for copy in sent:
        copy.wait_send()
    store.wait()


def shards(n_orb, integrals, coefficients, metric, screening):
    n = len(CHUNKS)
    dma = pltpu.SemaphoreType.DMA
    hbm = pl.BlockSpec(memory_space=pl.ANY)
    return pl.pallas_call(
        functools.partial(kernel, n_orb),
        out_shape=jax.ShapeDtypeStruct((64, 192), F32),
        in_specs=[hbm, hbm, pl.BlockSpec(memory_space=pltpu.VMEM), pl.BlockSpec(memory_space=pltpu.SMEM)],
        out_specs=hbm,
        scratch_shapes=[
            pltpu.VMEM((16, 64, 192), BF16),
            pltpu.VMEM((5, 64, 1024), BF16),
            pltpu.VMEM((6, 1024, 128), BF16),
            pltpu.VMEM((512, 1024), BF16),
            pltpu.VMEM((6, 256, 128), F32),
            pltpu.VMEM((6, 256, 128), F32),
            pltpu.VMEM((6, 256, 128), BF16),
            pltpu.VMEM((6, 256, 128), BF16),
            pltpu.VMEM((2, 6, 256, 128), BF16),
            pltpu.VMEM((2, 256, 768), BF16),
            pltpu.VMEM((2, 256, 768), BF16),
            pltpu.VMEM((3, 128, 2048), BF16),
            pltpu.VMEM((3, 256, 2048), BF16),
            pltpu.VMEM((64, 192), F32),
            pltpu.VMEM((7, 8, 192), F32),
            pltpu.VMEM((64, 192), F32),
            dma((4,)), dma((n, 4)), dma((n, 4)), dma((n,)), dma((n,)), dma((4,)), dma((4,)),
            dma((n, 2)), dma((n, 2)), dma((7,)), dma((7,)), dma((7,)), dma((7,)),
        ],
        compiler_params=pltpu.CompilerParams(
            collective_id=0, has_side_effects=True, vmem_limit_bytes=48 * 1024 * 1024
        ),
    )(integrals, coefficients, metric, screening)


def solution(mesh):
    in_specs = (P("aux", "orb", None), P("orb", None), P(), P("aux", "orb", None))
    body = functools.partial(shards, mesh.shape["orb"])
    return jax.shard_map(body, mesh=mesh, in_specs=in_specs, out_specs=P("orb", None), check_vma=False)
```

```python
import functools

import jax
import jax.numpy as jnp
from jax import lax
from jax.experimental import pallas as pl
from jax.experimental.pallas import tpu as pltpu
from jax.sharding import PartitionSpec as P

MESH = pl.DeviceIdType.MESH
F32 = jnp.float32
BF16 = jnp.bfloat16
HEAD = (0, 4, 2, 5)
TAIL = (1, 3)
CHUNKS = tuple((t, 1) for t in range(6))


def nn(a, b):
    return lax.dot_general(a, b, (((1,), (0,)), ((), ())), preferred_element_type=F32)


def nt(a, b):
    return lax.dot_general(a, b, (((1,), (1,)), ((), ())), preferred_element_type=F32)


def split(x):
    high = x.astype(BF16)
    return high, (x - high.astype(F32)).astype(BF16)


def iota(shape, dim):
    return lax.broadcasted_iota(jnp.int32, shape, dim)


def fold(x):
    return jnp.concatenate([x[16 * p : 16 * p + 16] for p in range(16)], axis=1)


def kernel(
    n_orb,
    a_ref, c_ref, metric_ref, screen_ref, o_ref,
    av, m_ref, s_ref, cb, ag, mk, psend, precv, ghi, glo, gn, sp_hi, sp_lo, hh, ht, kp, kr, quad, ob,
    load_sem, ag_send, ag_recv, sib_send, sib_recv, c_send, c_recv, g_send, g_recv, r_send, r_recv, b_send, b_recv,
):
    orb = lax.axis_index("orb")
    aux = lax.axis_index("aux")
    y = lax.div(aux, 2)
    core = lax.rem(aux, 2)
    sibling = (orb, 2 * y + 1 - core)
    up = (orb, lax.rem(aux + 2, 8))
    down = (orb, lax.rem(aux + 6, 8))
    after = (lax.rem(orb + 1, n_orb), aux)
    before = (lax.rem(orb + n_orb - 1, n_orb), aux)
    across = (orb, lax.rem(aux + 4, 8))

    def remote(src, dst, send, recv, target):
        return pltpu.make_async_remote_copy(
            src_ref=src, dst_ref=dst, send_sem=send, recv_sem=recv, device_id=target, device_id_type=MESH
        )

    load_a0 = pltpu.make_async_copy(a_ref.at[:, pl.ds(0, 32), :], av.at[:, pl.ds(0, 32), :], load_sem.at[0])
    load_a1 = pltpu.make_async_copy(a_ref.at[:, pl.ds(32, 32), :], av.at[:, pl.ds(32, 32), :], load_sem.at[1])
    load_c = pltpu.make_async_copy(c_ref, cb.at[2], load_sem.at[2])
    load_s = pltpu.make_async_copy(screen_ref, s_ref, load_sem.at[3])
    load_m = pltpu.make_async_copy(metric_ref, m_ref, load_sem.at[4])
    load_s.start()
    load_a0.start()
    load_c.start()
    load_a1.start()
    load_m.start()

    barrier = pltpu.get_barrier_semaphore()
    for target in (sibling, up, down, across, after, before):
        pl.semaphore_signal(barrier, inc=1, device_id=target, device_id_type=MESH)

    load_s.wait()
    gate = [s_ref[0, 0, k].astype(F32) for k in range(3)]
    lane = iota((1, 128), 1)
    head_mask = jnp.where(lane < 64, gate[0], gate[1]).astype(BF16)
    rows = pl.ds(pl.multiple_of(256 * y, 256), 256)

    def pack_head(group):
        piece = av[:, 16 * group : 16 * group + 16, 0:128].reshape(256, 128)
        ag[HEAD[group], rows, :] = piece * head_mask

    def pack_tail(which):
        shape = (64, 128)
        low = jnp.where(iota(shape, 0) == iota(shape, 1), gate[2], 0.0).astype(BF16)
        high = jnp.where(iota(shape, 0) + 64 == iota(shape, 1), gate[2], 0.0).astype(BF16)
        first = av[:, 16 * which : 16 * which + 16, 128:192].reshape(256, 64)
        second = av[:, 16 * which + 32 : 16 * which + 48, 128:192].reshape(256, 64)
        ag[TAIL[which], rows, :] = (nn(first, low) + nn(second, high)).astype(BF16)

    load_a0.wait()
    load_a1.wait()
    pack_head(0)
    pl.semaphore_wait(barrier, 6)

    def slot(c, index, first, count):
        t, n = CHUNKS[c]
        return ag.at[pl.ds(t, n), pl.ds(pl.multiple_of(256 * index + first, 128), count), :]

    y_up, y_down = lax.rem(y + 1, 4), lax.rem(y + 3, 4)

    def own(c):
        block = slot(c, y, 0, 256)
        return [
            remote(block, block, ag_send.at[c, 0], ag_recv.at[c, 0], up),
            remote(block, block, ag_send.at[c, 1], ag_recv.at[c, 1], down),
        ]

    def relay(c):
        first, second = slot(c, y_down, 0, 128), slot(c, y_up, 128, 128)
        return [
            remote(first, first, ag_send.at[c, 2], ag_recv.at[c, 2], up),
            remote(second, second, ag_send.at[c, 3], ag_recv.at[c, 3], down),
        ]

    owns = [own(c) for c in range(len(CHUNKS))]
    relays = [relay(c) for c in range(len(CHUNKS))]

    def start(copies):
        for copy in copies:
            copy.start()

    def arrive(copies):
        for copy in copies:
            copy.wait_recv()

    coef = [
        remote(cb.at[2], cb.at[1], c_send.at[0], c_recv.at[0], after),
        remote(cb.at[2], cb.at[3], c_send.at[1], c_recv.at[1], before),
    ]
    coef_on = [
        remote(cb.at[1], cb.at[0], c_send.at[2], c_recv.at[2], after),
        remote(cb.at[3], cb.at[4], c_send.at[3], c_recv.at[3], before),
    ]
    start(owns[0])
    pack_tail(0)
    start(owns[1])
    load_c.wait()
    start(coef)
    pack_head(2)
    start(owns[2])
    pack_tail(1)
    pack_head(1)
    pack_head(3)
    load_m.wait()

    metric_rows = m_ref[pl.ds(pl.multiple_of(32 * y, 32), 32), :]
    column = iota((128, 1024), 1)
    wanted = (2 * (column // 256) + core) * 16 + (column // 16) % 16
    spread = jnp.where(iota((128, 1024), 0) == wanted, 1.0, 0.0).astype(BF16)
    for part in range(4):
        row = iota((128, 32), 0) + 128 * part
        holder = core if part < 2 else 1 - core
        pick = jnp.where(iota((128, 32), 1) == holder * 16 + (row // 16) % 16, 1.0, 0.0).astype(BF16)
        picked = nn(pick, metric_rows).astype(BF16)
        wide = nn(picked, spread)
        same = iota((128, 1024), 0) % 16 == iota((128, 1024), 1) % 16
        mk[128 * part : 128 * part + 128, :] = jnp.where(same, wide, 0.0).astype(BF16)

    def gram():
        arrive(coef_on)
        left = cb[1:4].reshape(192, 1024)
        for d in range(3):
            right = jnp.concatenate([cb[d], cb[d + 1], cb[d + 2], cb[d + 2]], axis=0)
            lanes = slice(256 * d, 256 * d + 256)
            zero = jnp.zeros((64, 256), BF16)
            for part, dst in zip(split(nt(left, right)), (sp_hi, sp_lo)):
                dst[0, 0:192, lanes] = part
                dst[0, 192:256, lanes] = zero
                dst[1, 0:128, lanes] = part[0:128]
                dst[1, 128:192, lanes] = zero
                dst[1, 192:256, lanes] = part[128:192]

    def sib(c):
        t, n = CHUNKS[c]
        tiles = pl.ds(t, n)
        return remote(psend.at[tiles], precv.at[tiles], sib_send.at[c], sib_recv.at[c], sibling)

    sibs = [sib(c) for c in range(len(CHUNKS))]

    def near(c):
        t, n = CHUNKS[c]
        tiles = pl.ds(t, n)
        return [
            remote(ghi.at[tiles], gn.at[0, tiles], g_send.at[c, 0], g_recv.at[c, 0], after),
            remote(ghi.at[tiles], gn.at[1, tiles], g_send.at[c, 1], g_recv.at[c, 1], before),
        ]

    nears = [near(c) for c in range(len(CHUNKS))]
    kept = {}

    def mix(c):
        t, n = CHUNKS[c]
        arrive(relays[c])
        panel = jnp.concatenate([ag[i] for i in range(t, t + n)], axis=1)
        other = nn(mk[256:512, :], panel)
        for i in range(n):
            psend[t + i] = other[:, 128 * i : 128 * i + 128]
        sibs[c].start()
        mine = nn(mk[0:256, :], panel)
        kept[c] = mine

    def finish(c):
        t, n = CHUNKS[c]
        sibs[c].wait_recv()
        for i in range(n):
            high, low = split(kept[c][:, 128 * i : 128 * i + 128] + precv[t + i])
            ghi[t + i] = high
            glo[t + i] = low
        start(nears[c])

    low_lanes = iota((256, 128), 1) < 64

    def transform(group):
        par, h, t = group // 2, HEAD[group], TAIL[group % 2]
        high = jnp.concatenate([ghi[h], ghi[t]], axis=1)
        low = jnp.concatenate([glo[h], glo[t]], axis=1)
        for d in range(3):
            lanes = slice(256 * d, 256 * d + 256)
            right = sp_hi[par, :, lanes]
            out = nn(high, right) + nn(low, right) + nn(high, sp_lo[par, :, lanes])
            for at, part in enumerate(split(out)):
                row = slice(64 * at + 16 * group, 64 * at + 16 * group + 16)
                hh[d, row, :] = fold(part[:, 0:128])
                end = part[:, 128:256]
                zero = jnp.zeros_like(end)
                ht[d, row, :] = fold(jnp.where(low_lanes, end, zero))
                row = slice(128 + row.start, 128 + row.stop)
                ht[d, row, :] = fold(jnp.where(low_lanes, zero, end))

    def panel_of(ref, tiles):
        return jnp.concatenate([fold(ref[t]) for t in tiles], axis=0)

    def heads(d, ref, tiles):
        out = nt(hh[d], panel_of(ref, tiles))
        return out[0:64] + out[64:128]

    def tails(d, ref):
        out = nt(ht[d], panel_of(ref, TAIL))
        return out[0:64] + out[64:128], out[128:192] + out[192:256]

    arrive(owns[0])
    start(relays[0])
    start(owns[3])
    arrive(owns[1])
    start(relays[1])
    start(owns[4])
    arrive(coef)
    start(coef_on)
    arrive(owns[2])
    start(relays[2])
    start(owns[5])
    mix(0)
    arrive(owns[3])
    start(relays[3])
    finish(0)
    mix(1)
    arrive(owns[4])
    start(relays[4])
    mix(2)
    finish(1)
    arrive(owns[5])
    start(relays[5])
    finish(2)
    gram()
    mix(3)
    mix(4)
    finish(3)
    mix(5)
    finish(4)
    transform(0)
    finish(5)
    transform(2)
    transform(1)
    transform(3)

    bands = [None, None, None]
    even, odd = tails(1, ghi)
    first = heads(1, ghi, HEAD[:2]) + even + nt(hh[1, 0:64, :], panel_of(glo, HEAD[:2]))
    second = heads(1, ghi, HEAD[2:]) + odd + nt(hh[1, 0:64, :], panel_of(glo, HEAD[2:]))
    first = first + nt(ht[1, 0:64, :], panel_of(glo, TAIL))
    second = second + nt(ht[1, 128:192, :], panel_of(glo, TAIL))
    bands[1] = (first, second)
    for c in range(5):
        arrive(nears[c])
    partial = {}
    for d, ref in ((0, gn.at[0]), (2, gn.at[1])):
        even, odd = tails(d, ref)
        partial[d] = (heads(d, ref, HEAD[:2]) + even, heads(d, ref, HEAD[2:3]), odd)
    arrive(nears[5])
    for d, ref in ((0, gn.at[0]), (2, gn.at[1])):
        done, third, odd = partial[d]
        bands[d] = (done, jnp.concatenate([third, heads(d, ref, HEAD[3:])], axis=1) + odd)
    kp[0:64, :] = jnp.concatenate(bands[0] + bands[1], axis=1)
    last = jnp.concatenate(bands[2], axis=1)
    kp[64:96, :] = jnp.concatenate([last[0:32], last[32:64]], axis=1)

    mine = pl.ds(pl.multiple_of(48 * core, 16), 48)
    other = pl.ds(pl.multiple_of(48 * (1 - core), 16), 48)
    pair = remote(kp.at[other, :], kr, r_send.at[0], r_recv.at[0], sibling)
    pair.start()
    pair.wait_recv()
    quad[y] = kp[mine, :] + kr[...]
    gather = []
    for j, target in enumerate((up, down, across)):
        gather.append(remote(quad.at[y], quad.at[y], b_send.at[j], b_recv.at[j], target))
    start(gather)
    arrive(gather)
    ob[mine, :] = (quad[0] + quad[1]) + (quad[2] + quad[3])
    share = remote(ob.at[mine, :], ob.at[mine, :], r_send.at[1], r_recv.at[1], sibling)
    share.start()
    share.wait_recv()
    pair.wait_send()
    end = ob[64:96, :]
    right = jnp.concatenate([end[:, 0:64], end[:, 64:128]], axis=0)
    o_ref[...] = jnp.concatenate([ob[0:64, :], right], axis=1)
    sent = coef + coef_on + sibs + gather + [share]
    for copies in owns + relays + nears:
        sent = sent + copies
    for copy in sent:
        copy.wait_send()


def shards(n_orb, integrals, coefficients, metric, screening):
    n = len(CHUNKS)
    dma = pltpu.SemaphoreType.DMA
    hbm = pl.BlockSpec(memory_space=pltpu.HBM)
    return pl.pallas_call(
        functools.partial(kernel, n_orb),
        out_shape=jax.ShapeDtypeStruct((64, 192), F32),
        in_specs=[hbm, hbm, hbm, hbm],
        out_specs=pl.BlockSpec(memory_space=pltpu.VMEM),
        scratch_shapes=[
            pltpu.VMEM((16, 64, 192), BF16),
            pltpu.VMEM((128, 128), BF16),
            pltpu.SMEM((1, 1, 3), jnp.int32),
            pltpu.VMEM((5, 64, 1024), BF16),
            pltpu.VMEM((6, 1024, 128), BF16),
            pltpu.VMEM((512, 1024), BF16),
            pltpu.VMEM((6, 256, 128), F32),
            pltpu.VMEM((6, 256, 128), F32),
            pltpu.VMEM((6, 256, 128), BF16),
            pltpu.VMEM((6, 256, 128), BF16),
            pltpu.VMEM((2, 6, 256, 128), BF16),
            pltpu.VMEM((2, 256, 768), BF16),
            pltpu.VMEM((2, 256, 768), BF16),
            pltpu.VMEM((3, 128, 2048), BF16),
            pltpu.VMEM((3, 256, 2048), BF16),
            pltpu.VMEM((96, 128), F32),
            pltpu.VMEM((48, 128), F32),
            pltpu.VMEM((4, 48, 128), F32),
            pltpu.VMEM((96, 128), F32),
            dma((5,)), dma((n, 4)), dma((n, 4)), dma((n,)), dma((n,)), dma((4,)), dma((4,)),
            dma((n, 2)), dma((n, 2)), dma((2,)), dma((2,)), dma((3,)), dma((3,)),
        ],
        compiler_params=pltpu.CompilerParams(
            collective_id=0, has_side_effects=True, vmem_limit_bytes=62 * 1024 * 1024
        ),
    )(integrals, coefficients, metric, screening)


def solution(mesh):
    in_specs = (P("aux", "orb", None), P("orb", None), P(), P("aux", "orb", None))
    body = functools.partial(shards, mesh.shape["orb"])
    return jax.shard_map(body, mesh=mesh, in_specs=in_specs, out_specs=P("orb", None), check_vma=False)
```

```python
import functools

import jax
import jax.numpy as jnp
from jax import lax
from jax.experimental import pallas as pl
from jax.experimental.pallas import tpu as pltpu
from jax.sharding import PartitionSpec as P

MESH = pl.DeviceIdType.MESH
F32 = jnp.float32
BF16 = jnp.bfloat16
HEAD = (0, 4, 2, 5)
TAIL = (1, 3)
CHUNKS = tuple((t, 1) for t in range(6))


def nn(a, b):
    return lax.dot_general(a, b, (((1,), (0,)), ((), ())), preferred_element_type=F32)


def nt(a, b):
    return lax.dot_general(a, b, (((1,), (1,)), ((), ())), preferred_element_type=F32)


def split(x):
    high = x.astype(BF16)
    return high, (x - high.astype(F32)).astype(BF16)


def iota(shape, dim):
    return lax.broadcasted_iota(jnp.int32, shape, dim)


def fold(x):
    return jnp.concatenate([x[16 * p : 16 * p + 16] for p in range(16)], axis=1)


def kernel(
    n_orb,
    a_ref, c_ref, metric_ref, screen_ref, o_ref,
    av, m_ref, s_ref, cb, ag, mk, psend, precv, ghi, glo, gn, sp_hi, sp_lo, hh, ht, kp, kr, quad, ob, late,
    load_sem, ag_send, ag_recv, sib_send, sib_recv, c_send, c_recv, g_send, g_recv, r_send, r_recv, b_send, b_recv,
):
    orb = lax.axis_index("orb")
    aux = lax.axis_index("aux")
    y = lax.div(aux, 2)
    core = lax.rem(aux, 2)
    sibling = (orb, 2 * y + 1 - core)
    up = (orb, lax.rem(aux + 2, 8))
    down = (orb, lax.rem(aux + 6, 8))
    after = (lax.rem(orb + 1, n_orb), aux)
    before = (lax.rem(orb + n_orb - 1, n_orb), aux)
    across = (orb, lax.rem(aux + 4, 8))
    peers = [(orb, lax.rem(aux + j, 8)) for j in range(1, 8)]

    def remote(src, dst, send, recv, target):
        return pltpu.make_async_remote_copy(
            src_ref=src, dst_ref=dst, send_sem=send, recv_sem=recv, device_id=target, device_id_type=MESH
        )

    load_a0 = pltpu.make_async_copy(a_ref.at[:, pl.ds(0, 32), :], av.at[:, pl.ds(0, 32), :], load_sem.at[0])
    load_a1 = pltpu.make_async_copy(a_ref.at[:, pl.ds(32, 32), :], av.at[:, pl.ds(32, 32), :], load_sem.at[1])
    load_c = pltpu.make_async_copy(c_ref, cb.at[2], load_sem.at[2])
    load_s = pltpu.make_async_copy(screen_ref, s_ref, load_sem.at[3])
    load_m = pltpu.make_async_copy(metric_ref, m_ref, load_sem.at[4])
    load_s.start()
    load_a0.start()
    load_c.start()
    load_a1.start()
    load_m.start()

    barrier = pltpu.get_barrier_semaphore()
    for target in peers + [after, before]:
        pl.semaphore_signal(barrier, inc=1, device_id=target, device_id_type=MESH)

    load_s.wait()
    gate = [s_ref[0, 0, k].astype(F32) for k in range(3)]
    lane = iota((1, 128), 1)
    head_mask = jnp.where(lane < 64, gate[0], gate[1]).astype(BF16)

    def pack_head(group):
        piece = av[:, 16 * group : 16 * group + 16, 0:128].reshape(256, 128)
        ag[HEAD[group], 0:256, :] = piece * head_mask

    def pack_tail(which):
        shape = (64, 128)
        low = jnp.where(iota(shape, 0) == iota(shape, 1), gate[2], 0.0).astype(BF16)
        high = jnp.where(iota(shape, 0) + 64 == iota(shape, 1), gate[2], 0.0).astype(BF16)
        first = av[:, 16 * which : 16 * which + 16, 128:192].reshape(256, 64)
        second = av[:, 16 * which + 32 : 16 * which + 48, 128:192].reshape(256, 64)
        ag[TAIL[which], 0:256, :] = (nn(first, low) + nn(second, high)).astype(BF16)

    load_a0.wait()
    load_a1.wait()
    pack_head(0)
    pl.semaphore_wait(barrier, 9)

    def slot(c, place, first, count):
        t, n = CHUNKS[c]
        return ag.at[pl.ds(t, n), pl.ds(256 * place + first, count), :]

    def own(c):
        block = slot(c, 0, 0, 256)
        return [
            remote(block, slot(c, 2, 0, 256), ag_send.at[c, 0], ag_recv.at[c, 0], up),
            remote(block, slot(c, 1, 0, 256), ag_send.at[c, 1], ag_recv.at[c, 1], down),
        ]

    def relay(c):
        return [
            remote(slot(c, 2, 0, 128), slot(c, 3, 0, 128), ag_send.at[c, 2], ag_recv.at[c, 2], up),
            remote(slot(c, 1, 128, 128), slot(c, 3, 128, 128), ag_send.at[c, 3], ag_recv.at[c, 3], down),
        ]

    owns = [own(c) for c in range(len(CHUNKS))]
    relays = [relay(c) for c in range(len(CHUNKS))]

    def start(copies):
        for copy in copies:
            copy.start()

    def arrive(copies):
        for copy in copies:
            copy.wait_recv()

    coef = [
        remote(cb.at[2], cb.at[1], c_send.at[0], c_recv.at[0], after),
        remote(cb.at[2], cb.at[3], c_send.at[1], c_recv.at[1], before),
    ]
    coef_on = [
        remote(cb.at[1], cb.at[0], c_send.at[2], c_recv.at[2], after),
        remote(cb.at[3], cb.at[4], c_send.at[3], c_recv.at[3], before),
    ]
    start(owns[0])
    pack_tail(0)
    start(owns[1])
    load_c.wait()
    start(coef)
    pack_head(2)
    start(owns[2])
    pack_tail(1)
    pack_head(1)
    pack_head(3)
    load_m.wait()

    metric_rows = m_ref[pl.ds(pl.multiple_of(32 * y, 32), 32), :]
    column = iota((128, 1024), 1)
    place = column // 256
    chip = (y + jnp.where(place < 2, place, 5 - place)) % 4
    wanted = (2 * chip + core) * 16 + (column // 16) % 16
    spread = jnp.where(iota((128, 1024), 0) == wanted, 1.0, 0.0).astype(BF16)
    for part in range(4):
        row = iota((128, 32), 0) + 128 * part
        holder = core if part < 2 else 1 - core
        pick = jnp.where(iota((128, 32), 1) == holder * 16 + (row // 16) % 16, 1.0, 0.0).astype(BF16)
        picked = nn(pick, metric_rows).astype(BF16)
        wide = nn(picked, spread)
        same = iota((128, 1024), 0) % 16 == iota((128, 1024), 1) % 16
        mk[128 * part : 128 * part + 128, :] = jnp.where(same, wide, 0.0).astype(BF16)

    def gram():
        arrive(coef_on)
        left = cb[1:4].reshape(192, 1024)
        for d in range(3):
            right = jnp.concatenate([cb[d], cb[d + 1], cb[d + 2], cb[d + 2]], axis=0)
            lanes = slice(256 * d, 256 * d + 256)
            zero = jnp.zeros((64, 256), BF16)
            for part, dst in zip(split(nt(left, right)), (sp_hi, sp_lo)):
                dst[0, 0:192, lanes] = part
                dst[0, 192:256, lanes] = zero
                dst[1, 0:128, lanes] = part[0:128]
                dst[1, 128:192, lanes] = zero
                dst[1, 192:256, lanes] = part[128:192]

    def sib(c):
        t, n = CHUNKS[c]
        tiles = pl.ds(t, n)
        return remote(psend.at[tiles], precv.at[tiles], sib_send.at[c], sib_recv.at[c], sibling)

    sibs = [sib(c) for c in range(len(CHUNKS))]

    def near(c):
        t, n = CHUNKS[c]
        tiles = pl.ds(t, n)
        return [
            remote(ghi.at[tiles], gn.at[0, tiles], g_send.at[c, 0], g_recv.at[c, 0], after),
            remote(ghi.at[tiles], gn.at[1, tiles], g_send.at[c, 1], g_recv.at[c, 1], before),
        ]

    nears = [near(c) for c in range(len(CHUNKS))]
    kept = {}

    early = {}

    def premix(c):
        t, n = CHUNKS[c]
        panel = jnp.concatenate([ag[i, 0:768, :] for i in range(t, t + n)], axis=1)
        early[c] = nn(mk[:, 0:768], panel)

    def mix(c):
        t, n = CHUNKS[c]
        arrive(relays[c])
        panel = jnp.concatenate([ag[i, 768:1024, :] for i in range(t, t + n)], axis=1)
        other = early[c][256:512] + nn(mk[256:512, 768:1024], panel)
        for i in range(n):
            psend[t + i] = other[:, 128 * i : 128 * i + 128]
        sibs[c].start()
        kept[c] = early[c][0:256] + nn(mk[0:256, 768:1024], panel)

    def finish(c):
        t, n = CHUNKS[c]
        sibs[c].wait_recv()
        for i in range(n):
            high, low = split(kept[c][:, 128 * i : 128 * i + 128] + precv[t + i])
            ghi[t + i] = high
            glo[t + i] = low
        start(nears[c])

    low_lanes = iota((256, 128), 1) < 64

    def transform(group):
        par, h, t = group // 2, HEAD[group], TAIL[group % 2]
        high = jnp.concatenate([ghi[h], ghi[t]], axis=1)
        low = jnp.concatenate([glo[h], glo[t]], axis=1)
        for d in range(3):
            lanes = slice(256 * d, 256 * d + 256)
            right = sp_hi[par, :, lanes]
            out = nn(high, right) + nn(low, right) + nn(high, sp_lo[par, :, lanes])
            for at, part in enumerate(split(out)):
                row = slice(64 * at + 16 * group, 64 * at + 16 * group + 16)
                hh[d, row, :] = fold(part[:, 0:128])
                end = part[:, 128:256]
                zero = jnp.zeros_like(end)
                ht[d, row, :] = fold(jnp.where(low_lanes, end, zero))
                row = slice(128 + row.start, 128 + row.stop)
                ht[d, row, :] = fold(jnp.where(low_lanes, zero, end))

    def panel_of(ref, tiles):
        return jnp.concatenate([fold(ref[t]) for t in tiles], axis=0)

    def heads(d, ref, tiles):
        out = nt(hh[d], panel_of(ref, tiles))
        return out[0:64] + out[64:128]

    def tails(d, ref):
        out = nt(ht[d], panel_of(ref, TAIL))
        return jnp.concatenate([out[0:64] + out[64:128], out[128:192] + out[192:256]], axis=1)

    def diagonal():
        out = nt(hh[1], jnp.concatenate([panel_of(ghi, HEAD), panel_of(glo, HEAD)], axis=0))
        head = out[0:64, 0:64] + out[64:128, 0:64] + out[0:64, 64:128]
        out = nt(ht[1], jnp.concatenate([panel_of(ghi, TAIL), panel_of(glo, TAIL)], axis=0))
        even = out[0:64, 0:32] + out[64:128, 0:32] + out[0:64, 32:64]
        odd = out[128:192, 0:32] + out[192:256, 0:32] + out[128:192, 32:64]
        return head + jnp.concatenate([even, odd], axis=1)

    arrive(owns[0])
    start(relays[0])
    start(owns[3])
    premix(0)
    arrive(owns[1])
    start(relays[1])
    start(owns[4])
    premix(1)
    arrive(coef)
    start(coef_on)
    arrive(owns[2])
    start(relays[2])
    start(owns[5])
    premix(2)
    mix(0)
    arrive(owns[3])
    start(relays[3])
    premix(3)
    mix(1)
    finish(0)
    arrive(owns[4])
    start(relays[4])
    premix(4)
    mix(2)
    finish(1)
    gram()
    arrive(owns[5])
    start(relays[5])
    finish(2)
    premix(5)
    mix(3)
    transform(0)
    mix(4)
    finish(3)
    mix(5)
    finish(4)
    transform(2)
    finish(5)
    transform(1)
    transform(3)

    bands = [None, diagonal(), None]
    for c in range(4):
        arrive(nears[c])
    blank = jnp.zeros((64, 16), F32)
    for d, ref in ((0, gn.at[0]), (2, gn.at[1])):
        out = heads(d, ref, HEAD[0::2])
        bands[d] = jnp.concatenate([out[:, 0:16], blank, out[:, 16:32], blank], axis=1) + tails(d, ref)
    kp[0:64, :] = jnp.concatenate(bands[:2], axis=1)
    kp[64:96, :] = jnp.concatenate([bands[2][0:32], bands[2][32:64]], axis=1)

    mine = pl.ds(pl.multiple_of(48 * core, 16), 48)
    other = pl.ds(pl.multiple_of(48 * (1 - core), 16), 48)
    pair = remote(kp.at[other, :], kr, r_send.at[0], r_recv.at[0], sibling)
    pair.start()
    pair.wait_recv()
    quad[y] = kp[mine, :] + kr[...]
    gather = []
    for j, target in enumerate((up, down, across)):
        gather.append(remote(quad.at[y], quad.at[y], b_send.at[j], b_recv.at[j], target))
    start(gather)

    arrive(nears[4])
    arrive(nears[5])
    end = jnp.concatenate([heads(0, gn.at[0], HEAD[1::2]), heads(2, gn.at[1], HEAD[1::2])], axis=1)
    late[aux] = jnp.concatenate([end[0:32], end[32:64]], axis=1)
    for j, target in enumerate(peers):
        gather.append(remote(late.at[aux], late.at[aux], b_send.at[3 + j], b_recv.at[3 + j], target))
    start(gather[3:])
    arrive(gather[:3])
    ob[mine, :] = (quad[0] + quad[1]) + (quad[2] + quad[3])
    share = remote(ob.at[mine, :], ob.at[mine, :], r_send.at[1], r_recv.at[1], sibling)
    share.start()
    arrive(gather[3:])
    total = late[0]
    for j in range(1, 8):
        total = total + late[j]
    end = jnp.concatenate([total[:, 0:64], total[:, 64:128]], axis=0)
    left, right = [end[:, 16 * j : 16 * j + 16] for j in range(2)], [end[:, 32 + 16 * j : 48 + 16 * j] for j in range(2)]
    gap = jnp.zeros((64, 64), F32)
    ends = jnp.concatenate([blank, left[0], blank, left[1], gap, blank, right[0], blank, right[1]], axis=1)
    share.wait_recv()
    pair.wait_send()
    right = jnp.concatenate([ob[64:96, 0:64], ob[64:96, 64:128]], axis=0)
    o_ref[...] = jnp.concatenate([ob[0:64, :], right], axis=1) + ends
    sent = coef + coef_on + sibs + gather + [share]
    for copies in owns + relays + nears:
        sent = sent + copies
    for copy in sent:
        copy.wait_send()


def shards(n_orb, integrals, coefficients, metric, screening):
    n = len(CHUNKS)
    dma = pltpu.SemaphoreType.DMA
    hbm = pl.BlockSpec(memory_space=pltpu.HBM)
    return pl.pallas_call(
        functools.partial(kernel, n_orb),
        out_shape=jax.ShapeDtypeStruct((64, 192), F32),
        in_specs=[hbm, hbm, hbm, hbm],
        out_specs=pl.BlockSpec(memory_space=pltpu.VMEM),
        scratch_shapes=[
            pltpu.VMEM((16, 64, 192), BF16),
            pltpu.VMEM((128, 128), BF16),
            pltpu.SMEM((1, 1, 3), jnp.int32),
            pltpu.VMEM((5, 64, 1024), BF16),
            pltpu.VMEM((6, 1024, 128), BF16),
            pltpu.VMEM((512, 1024), BF16),
            pltpu.VMEM((6, 256, 128), F32),
            pltpu.VMEM((6, 256, 128), F32),
            pltpu.VMEM((6, 256, 128), BF16),
            pltpu.VMEM((6, 256, 128), BF16),
            pltpu.VMEM((2, 6, 256, 128), BF16),
            pltpu.VMEM((2, 256, 768), BF16),
            pltpu.VMEM((2, 256, 768), BF16),
            pltpu.VMEM((3, 128, 2048), BF16),
            pltpu.VMEM((3, 256, 2048), BF16),
            pltpu.VMEM((96, 128), F32),
            pltpu.VMEM((48, 128), F32),
            pltpu.VMEM((4, 48, 128), F32),
            pltpu.VMEM((96, 128), F32),
            pltpu.VMEM((8, 32, 128), F32),
            dma((5,)), dma((n, 4)), dma((n, 4)), dma((n,)), dma((n,)), dma((4,)), dma((4,)),
            dma((n, 2)), dma((n, 2)), dma((2,)), dma((2,)), dma((10,)), dma((10,)),
        ],
        compiler_params=pltpu.CompilerParams(
            collective_id=0, has_side_effects=True, vmem_limit_bytes=62 * 1024 * 1024
        ),
    )(integrals, coefficients, metric, screening)


def solution(mesh):
    in_specs = (P("aux", "orb", None), P("orb", None), P(), P("aux", "orb", None))
    body = functools.partial(shards, mesh.shape["orb"])
    return jax.shard_map(body, mesh=mesh, in_specs=in_specs, out_specs=P("orb", None), check_vma=False)
```

```python
import functools

import jax
import jax.numpy as jnp
from jax import lax
from jax.experimental import pallas as pl
from jax.experimental.pallas import tpu as pltpu
from jax.sharding import PartitionSpec as P

MESH = pl.DeviceIdType.MESH
F32 = jnp.float32
BF16 = jnp.bfloat16
HEAD = (0, 4, 2, 5)
TAIL = (1, 3)
CHUNKS = tuple((t, 1) for t in range(6))


def nn(a, b):
    return lax.dot_general(a, b, (((1,), (0,)), ((), ())), preferred_element_type=F32)


def nt(a, b):
    return lax.dot_general(a, b, (((1,), (1,)), ((), ())), preferred_element_type=F32)


def split(x):
    high = x.astype(BF16)
    return high, (x - high.astype(F32)).astype(BF16)


def iota(shape, dim):
    return lax.broadcasted_iota(jnp.int32, shape, dim)


def fold(x):
    return jnp.concatenate([x[16 * p : 16 * p + 16] for p in range(16)], axis=1)


def kernel(
    n_orb,
    a_ref, c_ref, metric_ref, screen_ref, o_ref,
    av, m_ref, s_ref, cb, ag, mk, psend, precv, ghi, glo, gn, sp_hi, sp_lo, hh, ht, kp, kr, quad, ob, late,
    load_sem, ag_send, ag_recv, sib_send, sib_recv, c_send, c_recv, g_send, g_recv, r_send, r_recv, b_send, b_recv,
):
    orb = lax.axis_index("orb")
    aux = lax.axis_index("aux")
    y = lax.div(aux, 2)
    core = lax.rem(aux, 2)
    sibling = (orb, 2 * y + 1 - core)
    up = (orb, lax.rem(aux + 2, 8))
    down = (orb, lax.rem(aux + 6, 8))
    after = (lax.rem(orb + 1, n_orb), aux)
    before = (lax.rem(orb + n_orb - 1, n_orb), aux)
    across = (orb, lax.rem(aux + 4, 8))
    peers = [(orb, lax.rem(aux + j, 8)) for j in range(1, 8)]

    def remote(src, dst, send, recv, target):
        return pltpu.make_async_remote_copy(
            src_ref=src, dst_ref=dst, send_sem=send, recv_sem=recv, device_id=target, device_id_type=MESH
        )

    load_a0 = pltpu.make_async_copy(a_ref.at[:, pl.ds(0, 32), :], av.at[:, pl.ds(0, 32), :], load_sem.at[0])
    load_a1 = pltpu.make_async_copy(a_ref.at[:, pl.ds(32, 32), :], av.at[:, pl.ds(32, 32), :], load_sem.at[1])
    load_c = pltpu.make_async_copy(c_ref, cb.at[2], load_sem.at[2])
    load_s = pltpu.make_async_copy(screen_ref, s_ref, load_sem.at[3])
    load_m = pltpu.make_async_copy(metric_ref, m_ref, load_sem.at[4])
    load_s.start()
    load_a0.start()
    load_c.start()
    load_a1.start()
    load_m.start()

    barrier = pltpu.get_barrier_semaphore()
    for target in peers + [after, before]:
        pl.semaphore_signal(barrier, inc=1, device_id=target, device_id_type=MESH)

    load_s.wait()
    gate = [s_ref[0, 0, k].astype(F32) for k in range(3)]
    lane = iota((1, 128), 1)
    head_mask = jnp.where(lane < 64, gate[0], gate[1]).astype(BF16)

    def pack_head(group):
        piece = av[:, 16 * group : 16 * group + 16, 0:128].reshape(256, 128)
        ag[HEAD[group], 0:256, :] = piece * head_mask

    def pack_tail(which):
        shape = (64, 128)
        low = jnp.where(iota(shape, 0) == iota(shape, 1), gate[2], 0.0).astype(BF16)
        high = jnp.where(iota(shape, 0) + 64 == iota(shape, 1), gate[2], 0.0).astype(BF16)
        first = av[:, 16 * which : 16 * which + 16, 128:192].reshape(256, 64)
        second = av[:, 16 * which + 32 : 16 * which + 48, 128:192].reshape(256, 64)
        ag[TAIL[which], 0:256, :] = (nn(first, low) + nn(second, high)).astype(BF16)

    load_a0.wait()
    load_a1.wait()
    pack_head(0)
    pl.semaphore_wait(barrier, 9)

    def slot(c, place, first, count):
        t, n = CHUNKS[c]
        return ag.at[pl.ds(t, n), pl.ds(256 * place + first, count), :]

    def own(c):
        block = slot(c, 0, 0, 256)
        return [
            remote(block, slot(c, 2, 0, 256), ag_send.at[c, 0], ag_recv.at[c, 0], up),
            remote(block, slot(c, 1, 0, 256), ag_send.at[c, 1], ag_recv.at[c, 1], down),
        ]

    def relay(c):
        return [
            remote(slot(c, 2, 0, 128), slot(c, 3, 0, 128), ag_send.at[c, 2], ag_recv.at[c, 2], up),
            remote(slot(c, 1, 128, 128), slot(c, 3, 128, 128), ag_send.at[c, 3], ag_recv.at[c, 3], down),
        ]

    owns = [own(c) for c in range(len(CHUNKS))]
    relays = [relay(c) for c in range(len(CHUNKS))]

    def start(copies):
        for copy in copies:
            copy.start()

    def arrive(copies):
        for copy in copies:
            copy.wait_recv()

    coef = [
        remote(cb.at[2], cb.at[1], c_send.at[0], c_recv.at[0], after),
        remote(cb.at[2], cb.at[3], c_send.at[1], c_recv.at[1], before),
    ]
    coef_on = [
        remote(cb.at[1], cb.at[0], c_send.at[2], c_recv.at[2], after),
        remote(cb.at[3], cb.at[4], c_send.at[3], c_recv.at[3], before),
    ]
    start(owns[0])
    pack_tail(0)
    start(owns[1])
    load_c.wait()
    start(coef)
    pack_head(2)
    start(owns[2])
    pack_tail(1)
    pack_head(1)
    pack_head(3)
    load_m.wait()

    metric_rows = m_ref[pl.ds(pl.multiple_of(32 * y, 32), 32), :]
    column = iota((128, 1024), 1)
    place = column // 256
    chip = (y + jnp.where(place < 2, place, 5 - place)) % 4
    wanted = (2 * chip + core) * 16 + (column // 16) % 16
    spread = jnp.where(iota((128, 1024), 0) == wanted, 1.0, 0.0).astype(BF16)
    for part in range(4):
        row = iota((128, 32), 0) + 128 * part
        holder = core if part < 2 else 1 - core
        pick = jnp.where(iota((128, 32), 1) == holder * 16 + (row // 16) % 16, 1.0, 0.0).astype(BF16)
        picked = nn(pick, metric_rows).astype(BF16)
        wide = nn(picked, spread)
        same = iota((128, 1024), 0) % 16 == iota((128, 1024), 1) % 16
        mk[128 * part : 128 * part + 128, :] = jnp.where(same, wide, 0.0).astype(BF16)

    def gram():
        arrive(coef_on)
        left = cb[1:4].reshape(192, 1024)
        for d in range(3):
            right = jnp.concatenate([cb[d], cb[d + 1], cb[d + 2], cb[d + 2]], axis=0)
            lanes = slice(256 * d, 256 * d + 256)
            zero = jnp.zeros((64, 256), BF16)
            for part, dst in zip(split(nt(left, right)), (sp_hi, sp_lo)):
                dst[0, 0:192, lanes] = part
                dst[0, 192:256, lanes] = zero
                dst[1, 0:128, lanes] = part[0:128]
                dst[1, 128:192, lanes] = zero
                dst[1, 192:256, lanes] = part[128:192]

    def sib(c):
        t, n = CHUNKS[c]
        tiles = pl.ds(t, n)
        return remote(psend.at[tiles], precv.at[tiles], sib_send.at[c], sib_recv.at[c], sibling)

    sibs = [sib(c) for c in range(len(CHUNKS))]

    def near(c):
        t, n = CHUNKS[c]
        tiles = pl.ds(t, n)
        return [
            remote(ghi.at[tiles], gn.at[0, tiles], g_send.at[c, 0], g_recv.at[c, 0], after),
            remote(ghi.at[tiles], gn.at[1, tiles], g_send.at[c, 1], g_recv.at[c, 1], before),
        ]

    nears = [near(c) for c in range(len(CHUNKS))]
    kept = {}

    early = {}

    def premix(c):
        t, n = CHUNKS[c]
        panel = jnp.concatenate([ag[i, 0:768, :] for i in range(t, t + n)], axis=1)
        early[c] = nn(mk[:, 0:768], panel)

    def mix(c):
        t, n = CHUNKS[c]
        arrive(relays[c])
        panel = jnp.concatenate([ag[i, 768:1024, :] for i in range(t, t + n)], axis=1)
        other = early[c][256:512] + nn(mk[256:512, 768:1024], panel)
        for i in range(n):
            psend[t + i] = other[:, 128 * i : 128 * i + 128]
        sibs[c].start()
        kept[c] = early[c][0:256] + nn(mk[0:256, 768:1024], panel)

    def finish(c):
        t, n = CHUNKS[c]
        sibs[c].wait_recv()
        for i in range(n):
            high, low = split(kept[c][:, 128 * i : 128 * i + 128] + precv[t + i])
            ghi[t + i] = high
            glo[t + i] = low
        start(nears[c])

    low_lanes = iota((256, 128), 1) < 64

    def transform(group):
        par, h, t = group // 2, HEAD[group], TAIL[group % 2]
        high = jnp.concatenate([ghi[h], ghi[t]], axis=1)
        low = jnp.concatenate([glo[h], glo[t]], axis=1)
        for d in range(3):
            lanes = slice(256 * d, 256 * d + 256)
            right = sp_hi[par, :, lanes]
            out = nn(high, right) + nn(low, right) + nn(high, sp_lo[par, :, lanes])
            for at, part in enumerate(split(out)):
                row = slice(64 * at + 16 * group, 64 * at + 16 * group + 16)
                hh[d, row, :] = fold(part[:, 0:128])
                end = part[:, 128:256]
                zero = jnp.zeros_like(end)
                ht[d, row, :] = fold(jnp.where(low_lanes, end, zero))
                row = slice(128 + row.start, 128 + row.stop)
                ht[d, row, :] = fold(jnp.where(low_lanes, zero, end))

    def panel_of(ref, tiles):
        return jnp.concatenate([fold(ref[t]) for t in tiles], axis=0)

    def heads(d, ref, tiles):
        out = nt(hh[d], panel_of(ref, tiles))
        return out[0:64] + out[64:128]

    def tails(d, ref):
        out = nt(ht[d], panel_of(ref, TAIL))
        return jnp.concatenate([out[0:64] + out[64:128], out[128:192] + out[192:256]], axis=1)

    def diagonal():
        out = nt(hh[1], jnp.concatenate([panel_of(ghi, HEAD), panel_of(glo, HEAD)], axis=0))
        head = out[0:64, 0:64] + out[64:128, 0:64] + out[0:64, 64:128]
        out = nt(ht[1], jnp.concatenate([panel_of(ghi, TAIL), panel_of(glo, TAIL)], axis=0))
        even = out[0:64, 0:32] + out[64:128, 0:32] + out[0:64, 32:64]
        odd = out[128:192, 0:32] + out[192:256, 0:32] + out[128:192, 32:64]
        return head + jnp.concatenate([even, odd], axis=1)

    arrive(owns[0])
    start(relays[0])
    start(owns[3])
    premix(0)
    arrive(owns[1])
    start(relays[1])
    start(owns[4])
    premix(1)
    arrive(coef)
    start(coef_on)
    arrive(owns[2])
    start(relays[2])
    start(owns[5])
    premix(2)
    mix(0)
    arrive(owns[3])
    start(relays[3])
    premix(3)
    mix(1)
    finish(0)
    arrive(owns[4])
    start(relays[4])
    premix(4)
    mix(2)
    finish(1)
    gram()
    arrive(owns[5])
    start(relays[5])
    finish(2)
    premix(5)
    mix(3)
    transform(0)
    mix(4)
    finish(3)
    mix(5)
    finish(4)
    transform(2)
    finish(5)
    transform(1)
    transform(3)

    bands = [None, diagonal(), None]
    for c in range(4):
        arrive(nears[c])
    blank = jnp.zeros((64, 16), F32)
    for d, ref in ((0, gn.at[0]), (2, gn.at[1])):
        out = heads(d, ref, HEAD[0::2])
        bands[d] = jnp.concatenate([out[:, 0:16], blank, out[:, 16:32], blank], axis=1) + tails(d, ref)
    kp[0:64, :] = jnp.concatenate(bands[:2], axis=1)
    kp[64:96, :] = jnp.concatenate([bands[2][0:32], bands[2][32:64]], axis=1)

    mine = pl.ds(pl.multiple_of(48 * core, 16), 48)
    other = pl.ds(pl.multiple_of(48 * (1 - core), 16), 48)
    pair = remote(kp.at[other, :], kr, r_send.at[0], r_recv.at[0], sibling)
    pair.start()
    pair.wait_recv()
    quad[y] = kp[mine, :] + kr[...]
    gather = []
    for j, target in enumerate((up, down, across)):
        gather.append(remote(quad.at[y], quad.at[y], b_send.at[j], b_recv.at[j], target))
    start(gather)

    arrive(nears[4])
    arrive(nears[5])
    end = jnp.concatenate([heads(0, gn.at[0], HEAD[1::2]), heads(2, gn.at[1], HEAD[1::2])], axis=1)
    late[aux] = jnp.concatenate([end[0:32], end[32:64]], axis=1)
    for j, target in enumerate(peers):
        gather.append(remote(late.at[aux], late.at[aux], b_send.at[3 + j], b_recv.at[3 + j], target))
    start(gather[3:])
    arrive(gather[:3])
    ob[mine, :] = (quad[0] + quad[1]) + (quad[2] + quad[3])
    share = remote(ob.at[mine, :], ob.at[mine, :], r_send.at[1], r_recv.at[1], sibling)
    share.start()
    arrive(gather[3:])
    total = late[0]
    for j in range(1, 8):
        total = total + late[j]
    end = jnp.concatenate([total[:, 0:64], total[:, 64:128]], axis=0)
    left, right = [end[:, 16 * j : 16 * j + 16] for j in range(2)], [end[:, 32 + 16 * j : 48 + 16 * j] for j in range(2)]
    gap = jnp.zeros((64, 64), F32)
    ends = jnp.concatenate([blank, left[0], blank, left[1], gap, blank, right[0], blank, right[1]], axis=1)
    share.wait_recv()
    pair.wait_send()
    right = jnp.concatenate([ob[64:96, 0:64], ob[64:96, 64:128]], axis=0)
    o_ref[...] = jnp.concatenate([ob[0:64, :], right], axis=1) + ends
    sent = coef + coef_on + sibs + gather + [share]
    for copies in owns + relays + nears:
        sent = sent + copies
    for copy in sent:
        copy.wait_send()


def shards(n_orb, integrals, coefficients, metric, screening):
    n = len(CHUNKS)
    dma = pltpu.SemaphoreType.DMA
    hbm = pl.BlockSpec(memory_space=pltpu.HBM)
    return pl.pallas_call(
        functools.partial(kernel, n_orb),
        out_shape=jax.ShapeDtypeStruct((64, 192), F32),
        in_specs=[hbm, hbm, hbm, hbm],
        out_specs=pl.BlockSpec(memory_space=pltpu.VMEM),
        scratch_shapes=[
            pltpu.VMEM((16, 64, 192), BF16),
            pltpu.VMEM((128, 128), BF16),
            pltpu.SMEM((1, 1, 3), jnp.int32),
            pltpu.VMEM((5, 64, 1024), BF16),
            pltpu.VMEM((6, 1024, 128), BF16),
            pltpu.VMEM((512, 1024), BF16),
            pltpu.VMEM((6, 256, 128), F32),
            pltpu.VMEM((6, 256, 128), F32),
            pltpu.VMEM((6, 256, 128), BF16),
            pltpu.VMEM((6, 256, 128), BF16),
            pltpu.VMEM((2, 6, 256, 128), BF16),
            pltpu.VMEM((2, 256, 768), BF16),
            pltpu.VMEM((2, 256, 768), BF16),
            pltpu.VMEM((3, 128, 2048), BF16),
            pltpu.VMEM((3, 256, 2048), BF16),
            pltpu.VMEM((96, 128), F32),
            pltpu.VMEM((48, 128), F32),
            pltpu.VMEM((4, 48, 128), F32),
            pltpu.VMEM((96, 128), F32),
            pltpu.VMEM((8, 32, 128), F32),
            dma((5,)), dma((n, 4)), dma((n, 4)), dma((n,)), dma((n,)), dma((4,)), dma((4,)),
            dma((n, 2)), dma((n, 2)), dma((2,)), dma((2,)), dma((10,)), dma((10,)),
        ],
        compiler_params=pltpu.CompilerParams(
            collective_id=0, has_side_effects=True, vmem_limit_bytes=48 * 1024 * 1024
        ),
    )(*[pltpu.with_memory_space_constraint(x, pltpu.HBM) for x in (integrals, coefficients, metric, screening)])


def solution(mesh):
    in_specs = (P("aux", "orb", None), P("orb", None), P(), P("aux", "orb", None))
    body = functools.partial(shards, mesh.shape["orb"])
    return jax.shard_map(body, mesh=mesh, in_specs=in_specs, out_specs=P("orb", None), check_vma=False)
```

```python
import functools

import jax
import jax.numpy as jnp
from jax import lax
from jax.experimental import pallas as pl
from jax.experimental.pallas import tpu as pltpu
from jax.sharding import PartitionSpec as P

MESH = pl.DeviceIdType.MESH
F32 = jnp.float32
BF16 = jnp.bfloat16
HEAD = (0, 4, 2, 5)
TAIL = (1, 3)
CHUNKS = tuple((t, 1) for t in range(6))


def nn(a, b):
    return lax.dot_general(a, b, (((1,), (0,)), ((), ())), preferred_element_type=F32)


def nt(a, b):
    return lax.dot_general(a, b, (((1,), (1,)), ((), ())), preferred_element_type=F32)


def split(x):
    high = x.astype(BF16)
    return high, (x - high.astype(F32)).astype(BF16)


def iota(shape, dim):
    return lax.broadcasted_iota(jnp.int32, shape, dim)


def fold(x):
    return jnp.concatenate([x[16 * p : 16 * p + 16] for p in range(16)], axis=1)


def kernel(
    n_orb,
    a_ref, c_ref, metric_ref, screen_ref, o_ref,
    av, m_ref, s_ref, cb, ag, mk, psend, precv, ghi, glo, gn, sp, hh, ht, kp, kr, quad, ob, late,
    load_sem, ag_send, ag_recv, sib_send, sib_recv, c_send, c_recv, g_send, g_recv, r_send, r_recv, b_send, b_recv,
):
    orb = lax.axis_index("orb")
    aux = lax.axis_index("aux")
    y = lax.div(aux, 2)
    core = lax.rem(aux, 2)
    sibling = (orb, 2 * y + 1 - core)
    up = (orb, lax.rem(aux + 2, 8))
    down = (orb, lax.rem(aux + 6, 8))
    after = (lax.rem(orb + 1, n_orb), aux)
    before = (lax.rem(orb + n_orb - 1, n_orb), aux)
    across = (orb, lax.rem(aux + 4, 8))
    peers = [(orb, lax.rem(aux + j, 8)) for j in range(1, 8)]

    def remote(src, dst, send, recv, target):
        return pltpu.make_async_remote_copy(
            src_ref=src, dst_ref=dst, send_sem=send, recv_sem=recv, device_id=target, device_id_type=MESH
        )

    load_a0 = pltpu.make_async_copy(a_ref.at[:, pl.ds(0, 32), :], av.at[:, pl.ds(0, 32), :], load_sem.at[0])
    load_a1 = pltpu.make_async_copy(a_ref.at[:, pl.ds(32, 32), :], av.at[:, pl.ds(32, 32), :], load_sem.at[1])
    load_c = pltpu.make_async_copy(c_ref, cb.at[2], load_sem.at[2])
    load_s = pltpu.make_async_copy(screen_ref, s_ref, load_sem.at[3])
    load_m = pltpu.make_async_copy(metric_ref, m_ref, load_sem.at[4])
    load_s.start()
    load_a0.start()
    load_c.start()
    load_a1.start()
    load_m.start()

    barrier = pltpu.get_barrier_semaphore()
    for target in peers + [after, before]:
        pl.semaphore_signal(barrier, inc=1, device_id=target, device_id_type=MESH)

    load_s.wait()
    gate = [s_ref[0, 0, k].astype(F32) for k in range(3)]
    lane = iota((1, 128), 1)
    head_mask = jnp.where(lane < 64, gate[0], gate[1]).astype(BF16)

    def pack_head(group):
        piece = av[:, 16 * group : 16 * group + 16, 0:128].reshape(256, 128)
        ag[HEAD[group], 0:256, :] = piece * head_mask

    def pack_tail(which):
        shape = (64, 128)
        low = jnp.where(iota(shape, 0) == iota(shape, 1), gate[2], 0.0).astype(BF16)
        high = jnp.where(iota(shape, 0) + 64 == iota(shape, 1), gate[2], 0.0).astype(BF16)
        first = av[:, 16 * which : 16 * which + 16, 128:192].reshape(256, 64)
        second = av[:, 16 * which + 32 : 16 * which + 48, 128:192].reshape(256, 64)
        ag[TAIL[which], 0:256, :] = (nn(first, low) + nn(second, high)).astype(BF16)

    load_a0.wait()
    load_a1.wait()
    pack_head(0)
    pl.semaphore_wait(barrier, 9)

    def slot(c, place, first, count):
        t, n = CHUNKS[c]
        return ag.at[pl.ds(t, n), pl.ds(256 * place + first, count), :]

    def own(c):
        block = slot(c, 0, 0, 256)
        return [
            remote(block, slot(c, 2, 0, 256), ag_send.at[c, 0], ag_recv.at[c, 0], up),
            remote(block, slot(c, 1, 0, 256), ag_send.at[c, 1], ag_recv.at[c, 1], down),
        ]

    def relay(c):
        return [
            remote(slot(c, 2, 0, 128), slot(c, 3, 0, 128), ag_send.at[c, 2], ag_recv.at[c, 2], up),
            remote(slot(c, 1, 128, 128), slot(c, 3, 128, 128), ag_send.at[c, 3], ag_recv.at[c, 3], down),
        ]

    owns = [own(c) for c in range(len(CHUNKS))]
    relays = [relay(c) for c in range(len(CHUNKS))]

    def start(copies):
        for copy in copies:
            copy.start()

    def arrive(copies):
        for copy in copies:
            copy.wait_recv()

    coef = [
        remote(cb.at[2], cb.at[1], c_send.at[0], c_recv.at[0], after),
        remote(cb.at[2], cb.at[3], c_send.at[1], c_recv.at[1], before),
    ]
    coef_on = [
        remote(cb.at[1], cb.at[0], c_send.at[2], c_recv.at[2], after),
        remote(cb.at[3], cb.at[4], c_send.at[3], c_recv.at[3], before),
    ]
    start(owns[0])
    pack_tail(0)
    start(owns[1])
    load_c.wait()
    start(coef)
    pack_head(2)
    start(owns[2])
    pack_tail(1)
    pack_head(1)
    pack_head(3)
    load_m.wait()

    metric_rows = m_ref[pl.ds(pl.multiple_of(32 * y, 32), 32), :]
    column = iota((128, 1024), 1)
    place = column // 256
    chip = (y + jnp.where(place < 2, place, 5 - place)) % 4
    wanted = (2 * chip + core) * 16 + (column // 16) % 16
    spread = jnp.where(iota((128, 1024), 0) == wanted, 1.0, 0.0).astype(BF16)
    for part in range(4):
        row = iota((128, 32), 0) + 128 * part
        holder = core if part < 2 else 1 - core
        pick = jnp.where(iota((128, 32), 1) == holder * 16 + (row // 16) % 16, 1.0, 0.0).astype(BF16)
        picked = nn(pick, metric_rows).astype(BF16)
        wide = nn(picked, spread)
        same = iota((128, 1024), 0) % 16 == iota((128, 1024), 1) % 16
        mk[128 * part : 128 * part + 128, :] = jnp.where(same, wide, 0.0).astype(BF16)

    def gram():
        arrive(coef_on)
        left = cb[1:4].reshape(192, 1024)
        for d in range(3):
            right = jnp.concatenate([cb[d], cb[d + 1], cb[d + 2], cb[d + 2]], axis=0)
            lanes = slice(256 * d, 256 * d + 256)
            zero = jnp.zeros((64, 256), BF16)
            high, low = split(nt(left, right))
            for part, first in ((high, 0), (high, 256), (low, 512)):
                sp[0, first : first + 192, lanes] = part
                sp[0, first + 192 : first + 256, lanes] = zero
                sp[1, first : first + 128, lanes] = part[0:128]
                sp[1, first + 128 : first + 192, lanes] = zero
                sp[1, first + 192 : first + 256, lanes] = part[128:192]

    def sib(c):
        t, n = CHUNKS[c]
        tiles = pl.ds(t, n)
        return remote(psend.at[tiles], precv.at[tiles], sib_send.at[c], sib_recv.at[c], sibling)

    sibs = [sib(c) for c in range(len(CHUNKS))]

    def near(c):
        t, n = CHUNKS[c]
        tiles = pl.ds(t, n)
        return [
            remote(ghi.at[tiles], gn.at[0, tiles], g_send.at[c, 0], g_recv.at[c, 0], after),
            remote(ghi.at[tiles], gn.at[1, tiles], g_send.at[c, 1], g_recv.at[c, 1], before),
        ]

    nears = [near(c) for c in range(len(CHUNKS))]
    kept = {}

    early = {}

    def premix(c):
        panel = jnp.concatenate([ag[c, 0:768, :], ag[c + 1, 0:768, :]], axis=1)
        out = nn(mk[:, 0:768], panel)
        early[c], early[c + 1] = out[:, 0:128], out[:, 128:256]

    def mix(c):
        t, n = CHUNKS[c]
        arrive(relays[c])
        panel = jnp.concatenate([ag[i, 768:1024, :] for i in range(t, t + n)], axis=1)
        other = early[c][256:512] + nn(mk[256:512, 768:1024], panel)
        for i in range(n):
            psend[t + i] = other[:, 128 * i : 128 * i + 128]
        sibs[c].start()
        kept[c] = early[c][0:256] + nn(mk[0:256, 768:1024], panel)

    def finish(c):
        t, n = CHUNKS[c]
        sibs[c].wait_recv()
        for i in range(n):
            high, low = split(kept[c][:, 128 * i : 128 * i + 128] + precv[t + i])
            ghi[t + i] = high
            glo[t + i] = low
        start(nears[c])

    low_lanes = iota((256, 128), 1) < 64

    def transform(group):
        par, h, t = group // 2, HEAD[group], TAIL[group % 2]
        left = jnp.concatenate([ghi[h], ghi[t], glo[h], glo[t], ghi[h], ghi[t]], axis=1)
        for d in range(3):
            lanes = slice(256 * d, 256 * d + 256)
            out = nn(left, sp[par, :, lanes])
            for at, part in enumerate(split(out)):
                row = slice(64 * at + 16 * group, 64 * at + 16 * group + 16)
                hh[d, row, :] = fold(part[:, 0:128])
                end = part[:, 128:256]
                zero = jnp.zeros_like(end)
                ht[d, row, :] = fold(jnp.where(low_lanes, end, zero))
                row = slice(128 + row.start, 128 + row.stop)
                ht[d, row, :] = fold(jnp.where(low_lanes, zero, end))

    def panel_of(ref, tiles):
        return jnp.concatenate([fold(ref[t]) for t in tiles], axis=0)

    def heads(d, ref, tiles):
        out = nt(hh[d], panel_of(ref, tiles))
        return out[0:64] + out[64:128]

    def tails(d, ref, which):
        out = nt(ht[d], panel_of(ref, TAIL[which : which + 1]))
        return jnp.concatenate([out[0:64] + out[64:128], out[128:192] + out[192:256]], axis=1)

    def diagonal():
        out = nt(hh[1], jnp.concatenate([panel_of(ghi, HEAD), panel_of(glo, HEAD)], axis=0))
        head = out[0:64, 0:64] + out[64:128, 0:64] + out[0:64, 64:128]
        out = nt(ht[1], jnp.concatenate([panel_of(ghi, TAIL), panel_of(glo, TAIL)], axis=0))
        even = out[0:64, 0:32] + out[64:128, 0:32] + out[0:64, 32:64]
        odd = out[128:192, 0:32] + out[192:256, 0:32] + out[128:192, 32:64]
        return head + jnp.concatenate([even, odd], axis=1)

    arrive(owns[0])
    start(relays[0])
    start(owns[3])
    arrive(owns[1])
    start(relays[1])
    start(owns[4])
    premix(0)
    arrive(coef)
    start(coef_on)
    arrive(owns[2])
    start(relays[2])
    start(owns[5])
    mix(0)
    arrive(owns[3])
    start(relays[3])
    premix(2)
    mix(1)
    finish(0)
    arrive(owns[4])
    start(relays[4])
    mix(2)
    finish(1)
    gram()
    arrive(owns[5])
    start(relays[5])
    finish(2)
    premix(4)
    mix(3)
    transform(0)
    mix(4)
    finish(3)
    mix(5)
    finish(4)
    transform(2)
    finish(5)
    transform(1)
    transform(3)

    middle = diagonal()
    for c in range(3):
        arrive(nears[c])
    sides = [heads(d, gn.at[d // 2], HEAD[0::2]) + tails(d, gn.at[d // 2], 0) for d in (0, 2)]
    kp[...] = jnp.concatenate([middle] + sides, axis=1)

    mine = pl.ds(pl.multiple_of(32 * core, 16), 32)
    other = pl.ds(pl.multiple_of(32 * (1 - core), 16), 32)
    pair = remote(kp.at[other, :], kr, r_send.at[0], r_recv.at[0], sibling)
    pair.start()
    pair.wait_recv()
    quad[y] = kp[mine, :] + kr[...]
    gather = []
    for j, target in enumerate((up, down, across)):
        gather.append(remote(quad.at[y], quad.at[y], b_send.at[j], b_recv.at[j], target))
    start(gather)

    arrive(nears[3])
    ends = [tails(d, gn.at[d // 2], 1) for d in (0, 2)]
    arrive(nears[4])
    arrive(nears[5])
    ends = [ends[d // 2] + heads(d, gn.at[d // 2], HEAD[1::2]) for d in (0, 2)]
    end = jnp.concatenate(ends, axis=1)
    late[aux] = jnp.concatenate([end[0:32], end[32:64]], axis=1)
    for j, target in enumerate(peers):
        gather.append(remote(late.at[aux], late.at[aux], b_send.at[3 + j], b_recv.at[3 + j], target))
    start(gather[3:])
    for copies in owns + relays + nears + [coef, coef_on, sibs, gather[:3], [pair]]:
        for copy in copies:
            copy.wait_send()
    arrive(gather[:3])
    ob[mine, :] = (quad[0] + quad[1]) + (quad[2] + quad[3])
    share = remote(ob.at[mine, :], ob.at[mine, :], r_send.at[1], r_recv.at[1], sibling)
    share.start()
    arrive(gather[3:])
    total = late[0]
    for j in range(1, 8):
        total = total + late[j]
    end = jnp.concatenate([total[:, 0:64], total[:, 64:128]], axis=0)
    share.wait_recv()
    full = ob[...]
    piece = lambda x, at: x[:, at : at + 16]
    low = [piece(full, 64), piece(end, 0), piece(full, 80), piece(end, 16)]
    high = [piece(full, 96), piece(end, 32), piece(full, 112), piece(end, 48)]
    o_ref[...] = jnp.concatenate(low + [full[:, 0:64]] + high, axis=1)
    for copy in gather[3:] + [share]:
        copy.wait_send()


def shards(n_orb, integrals, coefficients, metric, screening):
    n = len(CHUNKS)
    dma = pltpu.SemaphoreType.DMA
    hbm = pl.BlockSpec(memory_space=pltpu.HBM)
    return pl.pallas_call(
        functools.partial(kernel, n_orb),
        out_shape=jax.ShapeDtypeStruct((64, 192), F32),
        in_specs=[hbm, hbm, hbm, hbm],
        out_specs=pl.BlockSpec(memory_space=pltpu.VMEM),
        scratch_shapes=[
            pltpu.VMEM((16, 64, 192), BF16),
            pltpu.VMEM((128, 128), BF16),
            pltpu.SMEM((1, 1, 3), jnp.int32),
            pltpu.VMEM((5, 64, 1024), BF16),
            pltpu.VMEM((6, 1024, 128), BF16),
            pltpu.VMEM((512, 1024), BF16),
            pltpu.VMEM((6, 256, 128), F32),
            pltpu.VMEM((6, 256, 128), F32),
            pltpu.VMEM((6, 256, 128), BF16),
            pltpu.VMEM((6, 256, 128), BF16),
            pltpu.VMEM((2, 6, 256, 128), BF16),
            pltpu.VMEM((2, 768, 768), BF16),
            pltpu.VMEM((3, 128, 2048), BF16),
            pltpu.VMEM((3, 256, 2048), BF16),
            pltpu.VMEM((64, 128), F32),
            pltpu.VMEM((32, 128), F32),
            pltpu.VMEM((4, 32, 128), F32),
            pltpu.VMEM((64, 128), F32),
            pltpu.VMEM((8, 32, 128), F32),
            dma((5,)), dma((n, 4)), dma((n, 4)), dma((n,)), dma((n,)), dma((4,)), dma((4,)),
            dma((n, 2)), dma((n, 2)), dma((2,)), dma((2,)), dma((10,)), dma((10,)),
        ],
        compiler_params=pltpu.CompilerParams(
            collective_id=0, has_side_effects=True, vmem_limit_bytes=48 * 1024 * 1024
        ),
    )(*[pltpu.with_memory_space_constraint(x, pltpu.HBM) for x in (integrals, coefficients, metric, screening)])


def solution(mesh):
    in_specs = (P("aux", "orb", None), P("orb", None), P(), P("aux", "orb", None))
    body = functools.partial(shards, mesh.shape["orb"])
    return jax.shard_map(body, mesh=mesh, in_specs=in_specs, out_specs=P("orb", None), check_vma=False)
```

```python
import functools

import jax
import jax.numpy as jnp
from jax import lax
from jax.experimental import pallas as pl
from jax.experimental.pallas import tpu as pltpu
from jax.sharding import PartitionSpec as P

MESH = pl.DeviceIdType.MESH
F32 = jnp.float32
BF16 = jnp.bfloat16
HEAD = (0, 4, 2, 5)
TAIL = (1, 3)
CHUNKS = tuple((t, 1) for t in range(6))


def nn(a, b):
    return lax.dot_general(a, b, (((1,), (0,)), ((), ())), preferred_element_type=F32)


def nt(a, b):
    return lax.dot_general(a, b, (((1,), (1,)), ((), ())), preferred_element_type=F32)


def split(x):
    high = x.astype(BF16)
    return high, (x - high.astype(F32)).astype(BF16)


def iota(shape, dim):
    return lax.broadcasted_iota(jnp.int32, shape, dim)


def fold(x):
    return jnp.concatenate([x[16 * p : 16 * p + 16] for p in range(16)], axis=1)


def kernel(
    n_orb,
    a_ref, c_ref, metric_ref, screen_ref, o_ref,
    av, m_ref, s_ref, cb, ag, mk, psend, precv, ghi, glo, gn, sp, hh, ht, kp, kr, quad, ob, late,
    load_sem, ag_send, ag_recv, sib_send, sib_recv, c_send, c_recv, g_send, g_recv, r_send, r_recv, b_send, b_recv,
):
    orb = lax.axis_index("orb")
    aux = lax.axis_index("aux")
    y = lax.div(aux, 2)
    core = lax.rem(aux, 2)
    sibling = (orb, 2 * y + 1 - core)
    up = (orb, lax.rem(aux + 2, 8))
    down = (orb, lax.rem(aux + 6, 8))
    after = (lax.rem(orb + 1, n_orb), aux)
    before = (lax.rem(orb + n_orb - 1, n_orb), aux)
    across = (orb, lax.rem(aux + 4, 8))
    peers = [(orb, lax.rem(aux + j, 8)) for j in range(1, 8)]

    def remote(src, dst, send, recv, target):
        return pltpu.make_async_remote_copy(
            src_ref=src, dst_ref=dst, send_sem=send, recv_sem=recv, device_id=target, device_id_type=MESH
        )

    load_a0 = pltpu.make_async_copy(a_ref.at[:, pl.ds(0, 32), :], av.at[:, pl.ds(0, 32), :], load_sem.at[0])
    load_a1 = pltpu.make_async_copy(a_ref.at[:, pl.ds(32, 32), :], av.at[:, pl.ds(32, 32), :], load_sem.at[1])
    load_c = pltpu.make_async_copy(c_ref, cb.at[2], load_sem.at[2])
    load_s = pltpu.make_async_copy(screen_ref, s_ref, load_sem.at[3])
    load_m = pltpu.make_async_copy(metric_ref, m_ref, load_sem.at[4])
    load_s.start()
    load_a0.start()
    load_c.start()
    load_a1.start()
    load_m.start()

    barrier = pltpu.get_barrier_semaphore()
    for target in peers + [after, before]:
        pl.semaphore_signal(barrier, inc=1, device_id=target, device_id_type=MESH)

    load_s.wait()
    gate = [s_ref[0, 0, k].astype(F32) for k in range(3)]
    lane = iota((1, 128), 1)
    head_mask = jnp.where(lane < 64, gate[0], gate[1]).astype(BF16)

    def pack_head(group):
        piece = av[:, 16 * group : 16 * group + 16, 0:128].reshape(256, 128)
        ag[HEAD[group], 0:256, :] = piece * head_mask

    def pack_tail(which):
        shape = (64, 128)
        low = jnp.where(iota(shape, 0) == iota(shape, 1), gate[2], 0.0).astype(BF16)
        high = jnp.where(iota(shape, 0) + 64 == iota(shape, 1), gate[2], 0.0).astype(BF16)
        first = av[:, 16 * which : 16 * which + 16, 128:192].reshape(256, 64)
        second = av[:, 16 * which + 32 : 16 * which + 48, 128:192].reshape(256, 64)
        ag[TAIL[which], 0:256, :] = (nn(first, low) + nn(second, high)).astype(BF16)

    load_a0.wait()
    load_a1.wait()
    pack_head(0)
    pl.semaphore_wait(barrier, 9)

    def slot(c, place, first, count):
        t, n = CHUNKS[c]
        return ag.at[pl.ds(t, n), pl.ds(256 * place + first, count), :]

    def own(c):
        block = slot(c, 0, 0, 256)
        return [
            remote(block, slot(c, 2, 0, 256), ag_send.at[c, 0], ag_recv.at[c, 0], up),
            remote(block, slot(c, 1, 0, 256), ag_send.at[c, 1], ag_recv.at[c, 1], down),
        ]

    def relay(c):
        return [
            remote(slot(c, 2, 0, 128), slot(c, 3, 0, 128), ag_send.at[c, 2], ag_recv.at[c, 2], up),
            remote(slot(c, 1, 128, 128), slot(c, 3, 128, 128), ag_send.at[c, 3], ag_recv.at[c, 3], down),
        ]

    owns = [own(c) for c in range(len(CHUNKS))]
    relays = [relay(c) for c in range(len(CHUNKS))]

    def start(copies):
        for copy in copies:
            copy.start()

    def arrive(copies):
        for copy in copies:
            copy.wait_recv()

    coef = [
        remote(cb.at[2], cb.at[1], c_send.at[0], c_recv.at[0], after),
        remote(cb.at[2], cb.at[3], c_send.at[1], c_recv.at[1], before),
    ]
    coef_on = [
        remote(cb.at[1], cb.at[0], c_send.at[2], c_recv.at[2], after),
        remote(cb.at[3], cb.at[4], c_send.at[3], c_recv.at[3], before),
    ]
    start(owns[0])
    pack_tail(0)
    start(owns[1])
    load_c.wait()
    start(coef)
    pack_head(2)
    start(owns[2])
    pack_tail(1)
    pack_head(1)
    pack_head(3)
    load_m.wait()

    metric_rows = m_ref[pl.ds(pl.multiple_of(32 * y, 32), 32), :]
    column = iota((128, 1024), 1)
    place = column // 256
    chip = (y + jnp.where(place < 2, place, 5 - place)) % 4
    wanted = (2 * chip + core) * 16 + (column // 16) % 16
    spread = jnp.where(iota((128, 1024), 0) == wanted, 1.0, 0.0).astype(BF16)
    for part in range(4):
        row = iota((128, 32), 0) + 128 * part
        holder = core if part < 2 else 1 - core
        pick = jnp.where(iota((128, 32), 1) == holder * 16 + (row // 16) % 16, 1.0, 0.0).astype(BF16)
        picked = nn(pick, metric_rows).astype(BF16)
        wide = nn(picked, spread)
        same = iota((128, 1024), 0) % 16 == iota((128, 1024), 1) % 16
        mk[128 * part : 128 * part + 128, :] = jnp.where(same, wide, 0.0).astype(BF16)

    def gram():
        arrive(coef_on)
        left = cb[1:4].reshape(192, 1024)
        for d in range(3):
            right = jnp.concatenate([cb[d], cb[d + 1], cb[d + 2], cb[d + 2]], axis=0)
            lanes = slice(256 * d, 256 * d + 256)
            zero = jnp.zeros((64, 256), BF16)
            high, low = split(nt(left, right))
            for part, first in ((high, 0), (high, 256), (low, 512)):
                sp[0, first : first + 192, lanes] = part
                sp[0, first + 192 : first + 256, lanes] = zero
                sp[1, first : first + 128, lanes] = part[0:128]
                sp[1, first + 128 : first + 192, lanes] = zero
                sp[1, first + 192 : first + 256, lanes] = part[128:192]

    def sib(c):
        t, n = CHUNKS[c]
        tiles = pl.ds(t, n)
        return remote(psend.at[tiles], precv.at[tiles], sib_send.at[c], sib_recv.at[c], sibling)

    sibs = [sib(c) for c in range(len(CHUNKS))]

    def near(c):
        t, n = CHUNKS[c]
        tiles = pl.ds(t, n)
        return [
            remote(ghi.at[tiles], gn.at[0, tiles], g_send.at[c, 0], g_recv.at[c, 0], after),
            remote(ghi.at[tiles], gn.at[1, tiles], g_send.at[c, 1], g_recv.at[c, 1], before),
        ]

    nears = [near(c) for c in range(len(CHUNKS))]
    kept = {}

    early = {}

    def premix(c):
        panel = jnp.concatenate([ag[c, 0:768, :], ag[c + 1, 0:768, :]], axis=1)
        out = nn(mk[:, 0:768], panel)
        early[c], early[c + 1] = out[:, 0:128], out[:, 128:256]

    def mix(c):
        t, n = CHUNKS[c]
        arrive(relays[c])
        panel = jnp.concatenate([ag[i, 768:1024, :] for i in range(t, t + n)], axis=1)
        other = early[c][256:512] + nn(mk[256:512, 768:1024], panel)
        for i in range(n):
            psend[t + i] = other[:, 128 * i : 128 * i + 128]
        sibs[c].start()
        kept[c] = early[c][0:256] + nn(mk[0:256, 768:1024], panel)

    def finish(c):
        t, n = CHUNKS[c]
        sibs[c].wait_recv()
        for i in range(n):
            high, low = split(kept[c][:, 128 * i : 128 * i + 128] + precv[t + i])
            ghi[t + i] = high
            glo[t + i] = low
        start(nears[c])

    low_lanes = iota((256, 128), 1) < 64

    def transform(group):
        par, h, t = group // 2, HEAD[group], TAIL[group % 2]
        left = jnp.concatenate([ghi[h], ghi[t], glo[h], glo[t], ghi[h], ghi[t]], axis=1)
        for d in range(3):
            lanes = slice(256 * d, 256 * d + 256)
            out = nn(left, sp[par, :, lanes])
            for at, part in enumerate(split(out) if d == 1 else (out.astype(BF16),)):
                row = slice(64 * at + 16 * group, 64 * at + 16 * group + 16)
                hh[d, row, :] = fold(part[:, 0:128])
                end = part[:, 128:256]
                zero = jnp.zeros_like(end)
                ht[d, row, :] = fold(jnp.where(low_lanes, end, zero))
                row = slice(128 + row.start, 128 + row.stop)
                ht[d, row, :] = fold(jnp.where(low_lanes, zero, end))

    def panel_of(ref, tiles):
        return jnp.concatenate([fold(ref[t]) for t in tiles], axis=0)

    def heads(d, ref, tiles):
        return nt(hh[d, 0:64, :], panel_of(ref, tiles))

    def tails(d, ref, which):
        panel = panel_of(ref, TAIL[which : which + 1])
        return jnp.concatenate([nt(ht[d, 0:64, :], panel), nt(ht[d, 128:192, :], panel)], axis=1)

    def diagonal():
        out = nt(hh[1], jnp.concatenate([panel_of(ghi, HEAD), panel_of(glo, HEAD)], axis=0))
        head = out[0:64, 0:64] + out[64:128, 0:64] + out[0:64, 64:128]
        out = nt(ht[1], jnp.concatenate([panel_of(ghi, TAIL), panel_of(glo, TAIL)], axis=0))
        even = out[0:64, 0:32] + out[64:128, 0:32] + out[0:64, 32:64]
        odd = out[128:192, 0:32] + out[192:256, 0:32] + out[128:192, 32:64]
        return head + jnp.concatenate([even, odd], axis=1)

    arrive(owns[0])
    start(relays[0])
    start(owns[3])
    arrive(owns[1])
    start(relays[1])
    start(owns[4])
    premix(0)
    arrive(coef)
    start(coef_on)
    arrive(owns[2])
    start(relays[2])
    start(owns[5])
    mix(0)
    arrive(owns[3])
    start(relays[3])
    premix(2)
    mix(1)
    finish(0)
    arrive(owns[4])
    start(relays[4])
    mix(2)
    finish(1)
    gram()
    arrive(owns[5])
    start(relays[5])
    finish(2)
    premix(4)
    mix(3)
    transform(0)
    mix(4)
    finish(3)
    mix(5)
    finish(4)
    transform(2)
    finish(5)
    transform(1)
    transform(3)

    middle = diagonal()
    for c in range(3):
        arrive(nears[c])
    sides = [heads(d, gn.at[d // 2], HEAD[0::2]) + tails(d, gn.at[d // 2], 0) for d in (0, 2)]
    kp[...] = jnp.concatenate([middle] + sides, axis=1)

    mine = pl.ds(pl.multiple_of(32 * core, 16), 32)
    other = pl.ds(pl.multiple_of(32 * (1 - core), 16), 32)
    pair = remote(kp.at[other, :], kr, r_send.at[0], r_recv.at[0], sibling)
    pair.start()
    pair.wait_recv()
    quad[y] = kp[mine, :] + kr[...]
    gather = []
    for j, target in enumerate((up, down, across)):
        gather.append(remote(quad.at[y], quad.at[y], b_send.at[j], b_recv.at[j], target))
    start(gather)

    arrive(nears[3])
    ends = [tails(d, gn.at[d // 2], 1) for d in (0, 2)]
    arrive(nears[4])
    arrive(nears[5])
    ends = [ends[d // 2] + heads(d, gn.at[d // 2], HEAD[1::2]) for d in (0, 2)]
    end = jnp.concatenate(ends, axis=1)
    late[aux] = jnp.concatenate([end[0:32], end[32:64]], axis=1)
    for j, target in enumerate(peers):
        gather.append(remote(late.at[aux], late.at[aux], b_send.at[3 + j], b_recv.at[3 + j], target))
    start(gather[3:])
    for copies in owns + relays + nears + [coef, coef_on, sibs, gather[:3], [pair]]:
        for copy in copies:
            copy.wait_send()
    arrive(gather[:3])
    ob[mine, :] = (quad[0] + quad[1]) + (quad[2] + quad[3])
    share = remote(ob.at[mine, :], ob.at[mine, :], r_send.at[1], r_recv.at[1], sibling)
    share.start()
    arrive(gather[3:])
    total = late[0]
    for j in range(1, 8):
        total = total + late[j]
    end = jnp.concatenate([total[:, 0:64], total[:, 64:128]], axis=0)
    share.wait_recv()
    full = ob[...]
    piece = lambda x, at: x[:, at : at + 16]
    low = [piece(full, 64), piece(end, 0), piece(full, 80), piece(end, 16)]
    high = [piece(full, 96), piece(end, 32), piece(full, 112), piece(end, 48)]
    o_ref[...] = jnp.concatenate(low + [full[:, 0:64]] + high, axis=1)
    for copy in gather[3:] + [share]:
        copy.wait_send()


def shards(n_orb, integrals, coefficients, metric, screening):
    n = len(CHUNKS)
    dma = pltpu.SemaphoreType.DMA
    hbm = pl.BlockSpec(memory_space=pltpu.HBM)
    return pl.pallas_call(
        functools.partial(kernel, n_orb),
        out_shape=jax.ShapeDtypeStruct((64, 192), F32),
        in_specs=[hbm, hbm, hbm, hbm],
        out_specs=pl.BlockSpec(memory_space=pltpu.VMEM),
        scratch_shapes=[
            pltpu.VMEM((16, 64, 192), BF16),
            pltpu.VMEM((128, 128), BF16),
            pltpu.SMEM((1, 1, 3), jnp.int32),
            pltpu.VMEM((5, 64, 1024), BF16),
            pltpu.VMEM((6, 1024, 128), BF16),
            pltpu.VMEM((512, 1024), BF16),
            pltpu.VMEM((6, 256, 128), F32),
            pltpu.VMEM((6, 256, 128), F32),
            pltpu.VMEM((6, 256, 128), BF16),
            pltpu.VMEM((6, 256, 128), BF16),
            pltpu.VMEM((2, 6, 256, 128), BF16),
            pltpu.VMEM((2, 768, 768), BF16),
            pltpu.VMEM((3, 128, 2048), BF16),
            pltpu.VMEM((3, 256, 2048), BF16),
            pltpu.VMEM((64, 128), F32),
            pltpu.VMEM((32, 128), F32),
            pltpu.VMEM((4, 32, 128), F32),
            pltpu.VMEM((64, 128), F32),
            pltpu.VMEM((8, 32, 128), F32),
            dma((5,)), dma((n, 4)), dma((n, 4)), dma((n,)), dma((n,)), dma((4,)), dma((4,)),
            dma((n, 2)), dma((n, 2)), dma((2,)), dma((2,)), dma((10,)), dma((10,)),
        ],
        compiler_params=pltpu.CompilerParams(
            collective_id=0, has_side_effects=True, vmem_limit_bytes=48 * 1024 * 1024
        ),
    )(*[pltpu.with_memory_space_constraint(x, pltpu.HBM) for x in (integrals, coefficients, metric, screening)])


def solution(mesh):
    in_specs = (P("aux", "orb", None), P("orb", None), P(), P("aux", "orb", None))
    body = functools.partial(shards, mesh.shape["orb"])
    return jax.shard_map(body, mesh=mesh, in_specs=in_specs, out_specs=P("orb", None), check_vma=False)
```
